512 devices in a mesh: outer: 8 (over y, core), dp: 16 (over z), tensor: 4 (over x).
Axes of the slice: x: 4, y: 4, z: 16, core: 2. Of those that a mesh axis runs over, the one named last changes fastest.
Arguments:
- acts: bfloat16 [32768, 4096], P(('outer', 'dp'), 'tensor'), may hold values from -6 to 6
- out_grads: bfloat16 [32768, 4096], P(('outer', 'dp')), may hold values from -2.8125 to 2.8125
- error: float32 [8, 4096, 4096], P('outer', 'dp', 'tensor'), may hold values from -6 to 6
- q_warm: float32 [4096, 64], P('tensor'), may hold values from -0.09375 to 0.09375
Outputs:
- error_next: float32 [8, 4096, 4096], P('outer', 'dp', 'tensor')
- q_next: float32 [4096, 64], P('tensor')
The draws below stay inside these ranges and needn't reach their ends.
All inputs are finite; a program needn't handle non-finite values.
Results may differ from the reference program's by a relative error of at most 0.0003.
Values may be sent and summed in bfloat16 or wider, within the bound.
A program may use at most 64 MiB of HBM per device.

```python
import math
import jax
import jax.numpy as jnp
from jax import lax

ROWS = 4096
COLS = 4096
RANK = 64
TOK_DEV = 256
TOKENS = 32768
N_OUTER = 8
N_DP = 16


def draw_out_grads(key, part):
    key = jax.random.fold_in(key, 11)
    key_scale, key_base = jax.random.split(key, 2)
    row_scale = jnp.exp(jax.random.uniform(key_scale, (ROWS,), jnp.float32, 0.0, math.log(10.0)))
    order = jnp.arange(TOKENS, dtype=jnp.float32)
    rising = 1.0 + 2.0 * order / TOKENS
    base = jax.random.normal(key_base, (TOKENS, ROWS), jnp.float32)
    base = jnp.clip(base, -6.0, 6.0)
    values = base * row_scale[None, :] * rising[:, None] / math.sqrt(N_DP * TOK_DEV)
    return values.astype(jnp.bfloat16)


def steps_of(rng, shape, pieces, smallest, top_value):
    def one(position, blocks):
        draws = jax.random.uniform(jax.random.fold_in(jax.random.fold_in(rng, 6), position), (blocks,), jnp.float32, smallest / len(pieces), top_value / len(pieces))
        return jnp.repeat(jnp.exp(draws), shape[position] // blocks).reshape((-1,) + (1,) * (len(shape) - position - 1))

    gain = one(*pieces[0])
    for cut in pieces[1:]:
        gain = gain * one(*cut)
    return gain


def gaussian(stream_key, extent, spread, most, shards=(), kind=jnp.bfloat16):
    drawn = jax.random.normal(stream_key, extent, jnp.float32) * spread
    if len(shards) > 0:
        drawn = steps_of(stream_key, extent, shards, -0.22, 0.18) * drawn
    return jnp.clip(drawn, min=-most, max=most).astype(kind)


def setup_inputs(seed: int = 0) -> dict:
    keys = jax.random.split(jax.random.key(seed), 5)
    return {
        "acts": gaussian(keys[0], (TOKENS, COLS), 1.0, 6.0, ((0, 128), (1, 4))),
        "out_grads": draw_out_grads(jax.random.fold_in(keys[4], 71), 0),
        "error": gaussian(keys[2], (N_OUTER, ROWS, COLS), 1.0, 6.0, ((0, 8), (1, 16), (2, 4)), jnp.float32),
        "q_warm": gaussian(keys[3], (COLS, RANK), COLS ** -0.5, 0.09375, ((0, 4),), jnp.float32),
    }


def reference(acts, out_grads, error, q_warm):
    high = lax.Precision.HIGHEST
    inputs = acts.astype(jnp.float32).reshape(N_OUTER, -1, COLS)
    grads = out_grads.astype(jnp.float32).reshape(N_OUTER, -1, ROWS)
    merged = jnp.einsum('otr,otc->orc', grads, inputs, precision=high) + error
    p_mean = jnp.einsum('orc,ck->rk', merged, q_warm, precision=high) / N_OUTER
    gram = jnp.dot(p_mean.T, p_mean, precision=high)
    chol = jnp.linalg.cholesky(gram)
    p_hat = jax.scipy.linalg.solve_triangular(chol, p_mean.T, lower=True).T
    q_next = jnp.einsum('orc,rk->ck', merged, p_hat, precision=high) / N_OUTER
    approx = jnp.dot(p_hat, q_next.T, precision=high)
    return (merged - approx[None], q_next)
```

```python
import functools

import jax
import jax.numpy as jnp
from jax import lax
from jax.experimental import pallas as pl
from jax.experimental.pallas import tpu as pltpu
from jax.sharding import PartitionSpec as P

MESH = pl.DeviceIdType.MESH
F32 = jnp.float32
BF16 = jnp.bfloat16
HIGH = lax.Precision.HIGHEST
NN = (((1,), (0,)), ((), ()))
NT = (((1,), (1,)), ((), ()))
TN = (((0,), (0,)), ((), ()))


def dot(a, b, dims, precision=None):
    return lax.dot_general(a, b, dims, precision=precision, preferred_element_type=F32)


def split3(a):
    hi = a.astype(BF16)
    rest = a - hi.astype(F32)
    mid = rest.astype(BF16)
    low = (rest - mid.astype(F32)).astype(BF16)
    return jnp.concatenate([hi, mid, low], axis=0)


def dot3(a, b, dims):
    k = a.shape[0]
    full = dot(split3(a), b, dims)
    return (full[2 * k :] + full[k : 2 * k]) + full[:k]


class Exchange:
    def __init__(self, axis, n, stride, slots, sems):
        self.axis, self.n, self.stride, self.slots, self.sems = axis, n, stride, slots, sems

    def start(self, source):
        size = self.n * self.stride
        me = lax.axis_index(self.axis)

        def send(d, carry):
            to = lax.rem(me + d * self.stride, size)
            pltpu.make_async_remote_copy(
                src_ref=source(to),
                dst_ref=self.slots.at[d],
                send_sem=self.sems.at[0],
                recv_sem=self.sems.at[1],
                device_id={self.axis: to},
                device_id_type=MESH,
            ).start()
            return carry

        lax.fori_loop(1, self.n, send, 0)

    def _wait(self, which):
        arrived = self.slots.at[pl.ds(1, self.n - 1)]
        pltpu.make_async_copy(arrived, arrived, self.sems.at[which]).wait()

    def wait_recv(self):
        self._wait(1)

    def wait_send(self):
        self._wait(0)


class Reduce:
    def __init__(self, n_g, n_z, part, grs, zsrc, zrs, zag, gag, sems):
        self.n_g, self.n_z, self.part, self.zsrc = n_g, n_z, part, zsrc
        self.tiles, self.width = zsrc.shape[0], zsrc.shape[2]
        self.dup = n_z // self.tiles
        self.grs = Exchange("outer", n_g, 1, grs, sems.at[0])
        self.zrs = Exchange("dp", n_z, 1, zrs, sems.at[1])
        self.zag = Exchange("dp", self.tiles, self.dup, zag, sems.at[2])
        self.gag = Exchange("outer", n_g, 1, gag, sems.at[3])

    def scatter_outer(self):
        self.grs.start(lambda to: self.part.at[to])

    def scatter_dp(self):
        self.grs.wait_recv()
        me = lax.axis_index("outer")
        self.grs.slots[0] = self.part[me]
        total = self.grs.slots[me]
        for source in range(1, self.n_g):
            total = total + self.grs.slots[lax.rem(me + self.n_g - source, self.n_g)]
        for tile in range(self.tiles):
            self.zsrc[tile] = total[:, tile * self.width : (tile + 1) * self.width]
        self.zrs.start(lambda to: self.zsrc.at[to // self.dup])

    def gather_dp(self):
        self.zrs.wait_recv()
        me = lax.axis_index("dp")
        self.zrs.slots[0] = self.zsrc[me // self.dup]
        total = self.zrs.slots[me]
        for source in range(1, self.n_z):
            total = total + self.zrs.slots[lax.rem(me + self.n_z - source, self.n_z)]
        self.zag.slots[0] = total
        self.zag.start(lambda to: self.zag.slots.at[0])

    def gather_outer(self):
        self.zag.wait_recv()
        mine = lax.axis_index("dp") // self.dup
        for tile in range(self.tiles):
            block = self.zag.slots[lax.rem(mine + self.tiles - tile, self.tiles)]
            self.gag.slots[0, :, tile * self.width : (tile + 1) * self.width] = block
        self.gag.start(lambda to: self.gag.slots.at[0])

    def finish(self):
        self.gag.wait_recv()
        me = lax.axis_index("outer")
        return jnp.concatenate(
            [self.gag.slots[lax.rem(me + self.n_g - source, self.n_g)] for source in range(self.n_g)], axis=0
        )

    def drain(self):
        for exchange in (self.grs, self.zrs, self.zag, self.gag):
            exchange.wait_send()


def kernel(
    sizes,
    acts, dy, err, q,
    out, q_out,
    held, dyv, dyall, errv, qv, wex, pfull, elim, ut,
    part_p, grs_p, zsrc_p, zrs_p, zag_p, gag_p,
    part_u, grs_u, zsrc_u, zrs_u, zag_u, gag_u,
    loc, ring_send, ring_recv, dyz_sems, dyx_sems, wex_sems, px_sems, p_sems, u_sems,
):
    n_g, n_z, n_x = sizes
    z, x = lax.axis_index("dp"), lax.axis_index("tensor")
    tok, cols = acts.shape
    rows = dy.shape[1]
    rows_z, rows_x = rows // n_z, rows // n_x
    rank = q.shape[1]
    quarter, half = tok // n_x, tok // 2
    steps = n_z // 2

    loads = [
        pltpu.make_async_copy(src, dst, loc.at[i])
        for i, (src, dst) in enumerate(((acts, held.at[0]), (q, qv), (err, errv), (dy, dyv)))
    ]
    for load in loads:
        load.start()
    my_tokens = pl.ds(pl.multiple_of(x * quarter, quarter), quarter)
    own_dy = pltpu.make_async_copy(
        dy.at[my_tokens, pl.ds(pl.multiple_of(z * rows_z, rows_z), rows_z)], dyall.at[0, my_tokens, :], loc.at[4]
    )
    own_dy.start()

    barrier = pltpu.get_barrier_semaphore()
    for axis, n in (("dp", n_z), ("tensor", n_x), ("outer", n_g)):
        def greet(d, carry, axis=axis, n=n):
            to = lax.rem(lax.axis_index(axis) + d, n)
            pl.semaphore_signal(barrier, inc=1, device_id={axis: to}, device_id_type=MESH)
            return carry

        lax.fori_loop(1, n, greet, 0)
    pl.semaphore_wait(barrier, n_z + n_x + n_g - 3)

    def chunk(slot, c):
        return held.at[slot, pl.ds(c * half, half), :]

    def ring_copy(direction, s, c):
        here, there = (s, s + 1) if direction == 0 else ((n_z - s) % n_z, n_z - s - 1)
        to = lax.rem(z + (1 if direction == 0 else n_z - 1), n_z)
        return pltpu.make_async_remote_copy(
            src_ref=acts.at[pl.ds(c * half, half), :] if s == 0 else chunk(here, c),
            dst_ref=chunk(there, c),
            send_sem=ring_send.at[direction, s, c],
            recv_sem=ring_recv.at[direction, s, c],
            device_id={"dp": to},
            device_id_type=MESH,
        )

    def sends(s, c):
        return [ring_copy(direction, s, c) for direction in range(2) if s < steps - 1 or c == direction]

    for c in range(2):
        for copy in sends(0, c):
            copy.start()

    def send_dy(d, carry):
        to = lax.rem(z + d, n_z)
        pltpu.make_async_remote_copy(
            src_ref=dy.at[my_tokens, pl.ds(pl.multiple_of(to * rows_z, rows_z), rows_z)],
            dst_ref=dyall.at[d, my_tokens, :],
            send_sem=dyz_sems.at[0],
            recv_sem=dyz_sems.at[1],
            device_id={"dp": to},
            device_id_type=MESH,
        ).start()
        return carry

    lax.fori_loop(1, n_z, send_dy, 0)

    def wait_dyz(which):
        arrived = dyall.at[pl.ds(1, n_z - 1), pl.ds(0, quarter), :]
        pltpu.make_async_copy(arrived, arrived, dyz_sems.at[which]).wait()

    def send_dyx():
        wait_dyz(1)
        own_dy.wait()

        def send(d, carry):
            mine = dyall.at[:, my_tokens, :]
            pltpu.make_async_remote_copy(
                src_ref=mine,
                dst_ref=mine,
                send_sem=dyx_sems.at[0],
                recv_sem=dyx_sems.at[1],
                device_id={"tensor": lax.rem(x + d, n_x)},
                device_id_type=MESH,
            ).start()
            return carry

        lax.fori_loop(1, n_x, send, 0)

    def wait_dyx(which):
        arrived = dyall.at[:, pl.ds(0, quarter * (n_x - 1)), :]
        pltpu.make_async_copy(arrived, arrived, dyx_sems.at[which]).wait()

    p_sum = Reduce(n_g, n_z, part_p, grs_p, zsrc_p, zrs_p, zag_p, gag_p, p_sems)
    u_sum = Reduce(n_g, n_z, part_u, grs_u, zsrc_u, zrs_u, zag_u, gag_u, u_sems)
    w_exchange = Exchange("tensor", n_x, 1, wex, wex_sems)
    p_exchange = Exchange("tensor", n_x, 1, pfull, px_sems)
    row_quarter = (z * rows_z) // rows_x
    row_start = pl.multiple_of(lax.rem(z * rows_z, rows_x), 128)

    def by_group(a):
        return a.reshape(n_g, rank // n_g, a.shape[1])

    def start_w():
        for load in loads[:3]:
            load.wait()
        qt = qv[...].T
        wex[0, :, :tok] = dot3(qt, held[0], NT)
        wex[0, :, tok:] = dot(qt, errv[...], NT, HIGH)
        w_exchange.start(lambda to: wex.at[0])

    def start_p():
        w_exchange.wait_recv()
        loads[3].wait()
        total = wex[x]
        for source in range(1, n_x):
            total = total + wex[lax.rem(x + n_x - source, n_x)]
        mine = dyv[:, pl.ds(pl.multiple_of(x * rows_x, rows_x), rows_x)]
        part_p[...] = by_group(dot3(total[:, :tok], mine, NN))

        @pl.when(x == row_quarter)
        def _():
            part_p[:, :, pl.ds(row_start, rows_z)] += by_group(total[:, tok:])

        p_sum.scatter_outer()

    def gather_p():
        pfull[0] = p_sum.finish() * (1.0 / n_g)
        p_exchange.start(lambda to: pfull.at[0])

    def p_rows():
        return pfull[lax.rem(x + n_x - row_quarter, n_x), :, pl.ds(row_start, rows_z)]

    def start_u():
        p_exchange.wait_recv()
        vt = jnp.zeros((rank, tok), F32)
        gram = jnp.zeros((rank, rank), F32)
        for source in range(n_x):
            p = pfull[lax.rem(x + n_x - source, n_x)]
            vt += dot3(p, dyv[:, source * rows_x : (source + 1) * rows_x], NT)
            gram += dot(p, p, NT, HIGH)
        part_u[...] = by_group(dot3(vt, held[0], NN) + dot(p_rows(), errv[...], NN, HIGH))
        u_sum.scatter_outer()
        row = lax.broadcasted_iota(jnp.int32, (rank, rank), 0)
        col = lax.broadcasted_iota(jnp.int32, (rank, rank), 1)
        elim[:, :rank] = (row == col).astype(F32)
        elim[:, rank:] = gram

    def eliminate(first, last):
        row = lax.broadcasted_iota(jnp.int32, (rank, 2 * rank), 0)
        lane = lax.broadcasted_iota(jnp.int32, (rank, 2 * rank), 1)
        lane1 = lax.broadcasted_iota(jnp.int32, (1, 2 * rank), 1)

        def column(j, carry):
            whole = elim[...]
            pivot_row = elim[pl.ds(j, 1), :]
            pivot = jnp.sum(jnp.where(lane1 == rank + j, pivot_row, 0.0), axis=1, keepdims=True)
            scale = 1.0 / jnp.sqrt(pivot)
            pivot_row = pivot_row * scale
            factor = jnp.sum(jnp.where(lane == rank + j, whole, 0.0), axis=1, keepdims=True) * scale
            elim[...] = jnp.where(row > j, whole - factor * pivot_row, jnp.where(row == j, pivot_row, whole))
            return carry

        lax.fori_loop(first, last, column, 0)

    def finish_u():
        ut[...] = u_sum.finish()

    def correct():
        inverse = elim[:, :rank]
        qt = dot(inverse, ut[...], NN, HIGH) * (1.0 / n_g)
        pt = dot(inverse, p_rows(), NN, HIGH)
        ut[...] = qt
        pltpu.make_async_copy(ut, q_out, loc.at[0]).start()
        p_hi, q_hi = pt.astype(BF16), qt.astype(BF16)
        p_lo, q_lo = (pt - p_hi.astype(F32)).astype(BF16), (qt - q_hi.astype(F32)).astype(BF16)
        left = jnp.concatenate([p_hi, p_hi, p_lo], axis=0)
        right = jnp.concatenate([q_hi, q_lo, q_hi], axis=0)
        errv[...] -= dot(left, right, TN)

    def add(slot):
        errv[...] += dot(dyall[slot], held[slot], TN)

    def add_ring(*distances):
        for d in distances:
            for slot in sorted({d, (n_z - d) % n_z}):
                add(slot)

    last = 2 * steps - 1
    work = [
        (2, p_sum.scatter_dp),
        (3, p_sum.gather_dp),
        (4, p_sum.gather_outer),
        (5, gather_p),
        (5, send_dyx),
        (7, start_u),
        (8, u_sum.scatter_dp),
        (9, u_sum.gather_dp),
        (10, u_sum.gather_outer),
        (11, finish_u),
        (11, lambda: wait_dyx(1)),
    ]
    pieces = 5
    for i in range(pieces):
        work.append((9 + i, functools.partial(eliminate, rank * i // pieces, rank * (i + 1) // pieces)))
    work.append((12, lambda: add_ring(*range(0, steps // 2))))
    work.append((13, lambda: add_ring(*range(steps // 2, steps - 1))))
    work.append((14, correct))

    start_w()
    start_p()
    for t in range(2, last + 1):
        s, c = t // 2, t % 2
        for copy in sends(s - 1, c):
            copy.wait_recv()
        for copy in sends(s, c):
            copy.start()
        for at, do in work:
            if at == t or (t == last and at > last):
                do()
    add_ring(steps - 1)
    for c in range(2):
        for copy in sends(steps - 1, c):
            copy.wait_recv()
    add(steps)
    result = pltpu.make_async_copy(errv, out, loc.at[1])
    result.start()

    for s in range(steps):
        for c in range(2):
            for copy in sends(s, c):
                copy.wait_send()
    wait_dyz(0)
    wait_dyx(0)
    w_exchange.wait_send()
    p_exchange.wait_send()
    p_sum.drain()
    u_sum.drain()
    pltpu.make_async_copy(ut, q_out, loc.at[0]).wait()
    result.wait()


def local(sizes, acts, out_grads, error, q_warm):
    n_g, n_z, n_x = sizes
    tok, cols = acts.shape
    rows = out_grads.shape[1]
    rows_z, rows_x = rows // n_z, rows // n_x
    rank = q_warm.shape[1]
    group = rank // n_g

    def reduce_scratch(width):
        tile = max(128, width // n_z)
        return [
            pltpu.VMEM((n_g, group, width), F32),
            pltpu.VMEM((n_g, group, width), F32),
            pltpu.VMEM((width // tile, group, tile), F32),
            pltpu.VMEM((n_z, group, tile), F32),
            pltpu.VMEM((width // tile, group, tile), F32),
            pltpu.VMEM((n_g, group, width), F32),
        ]

    anywhere = pl.BlockSpec(memory_space=pl.ANY)
    dma = pltpu.SemaphoreType.DMA
    new_error, q_next = pl.pallas_call(
        functools.partial(kernel, sizes),
        out_shape=(
            jax.ShapeDtypeStruct((rows_z, cols), F32),
            jax.ShapeDtypeStruct((rank, cols), F32),
        ),
        in_specs=[anywhere] * 4,
        out_specs=(anywhere, anywhere),
        scratch_shapes=[
            pltpu.VMEM((n_z, tok, cols), BF16),
            pltpu.VMEM((tok, rows), BF16),
            pltpu.VMEM((n_z, tok, rows_z), BF16),
            pltpu.VMEM((rows_z, cols), F32),
            pltpu.VMEM((cols, rank), F32),
            pltpu.VMEM((n_x, rank, tok + rows_z), F32),
            pltpu.VMEM((n_x, rank, rows_x), F32),
            pltpu.VMEM((rank, 2 * rank), F32),
            pltpu.VMEM((rank, cols), F32),
            *reduce_scratch(rows_x),
            *reduce_scratch(cols),
            dma((5,)),
            dma((2, n_z // 2, 2)),
            dma((2, n_z // 2, 2)),
            dma((2,)),
            dma((2,)),
            dma((2,)),
            dma((2,)),
            dma((4, 2)),
            dma((4, 2)),
        ],
        compiler_params=pltpu.CompilerParams(
            collective_id=0, has_side_effects=True, vmem_limit_bytes=48 * 1024 * 1024
        ),
        cost_estimate=pl.CostEstimate(
            flops=2 * rows_z * cols * tok * n_z, bytes_accessed=2 * tok * (cols + rows) + 8 * rows_z * cols, transcendentals=0
        ),
        name="powersgd_step",
    )(acts, out_grads, error[0], q_warm)
    return new_error[None], q_next.T


def solution(mesh):
    sizes = (mesh.shape["outer"], mesh.shape["dp"], mesh.shape["tensor"])
    in_specs = (
        P(("outer", "dp"), "tensor"),
        P(("outer", "dp"), None),
        P("outer", "dp", "tensor"),
        P("tensor", None),
    )
    out_specs = (P("outer", "dp", "tensor"), P("tensor", None))
    return jax.shard_map(
        functools.partial(local, sizes), mesh=mesh, in_specs=in_specs, out_specs=out_specs, check_vma=False
    )
```

```python
import functools

import jax
import jax.numpy as jnp
from jax import lax
from jax.experimental import pallas as pl
from jax.experimental.pallas import tpu as pltpu
from jax.sharding import PartitionSpec as P

MESH = pl.DeviceIdType.MESH
VMEM = 62
CHUNKS = 4
RIGHT = 2
F32 = jnp.float32
BF16 = jnp.bfloat16
HIGH = lax.Precision.HIGHEST
NN = (((1,), (0,)), ((), ()))
NT = (((1,), (1,)), ((), ()))
TN = (((0,), (0,)), ((), ()))


def dot(a, b, dims, precision=None):
    return lax.dot_general(a, b, dims, precision=precision, preferred_element_type=F32)


def split3(a):
    hi = a.astype(BF16)
    rest = a - hi.astype(F32)
    mid = rest.astype(BF16)
    low = (rest - mid.astype(F32)).astype(BF16)
    return jnp.concatenate([hi, mid, low], axis=0)


def dot3(a, b, dims):
    k = a.shape[0]
    full = dot(split3(a), b, dims)
    return (full[2 * k :] + full[k : 2 * k]) + full[:k]


class Exchange:
    def __init__(self, axis, n, slots, sems):
        self.axis, self.n, self.slots, self.sems = axis, n, slots, sems

    def me(self):
        return lax.axis_index(self.axis)

    def get(self, source):
        return self.slots[lax.rem(self.me() + self.n - source, self.n)]

    def start(self, source):
        def send(d, carry):
            to = lax.rem(self.me() + d, self.n)
            pltpu.make_async_remote_copy(
                src_ref=source(to),
                dst_ref=self.slots.at[d],
                send_sem=self.sems.at[0],
                recv_sem=self.sems.at[1],
                device_id={self.axis: to},
                device_id_type=MESH,
            ).start()
            return carry

        lax.fori_loop(1, self.n, send, 0)

    def _wait(self, which):
        arrived = self.slots.at[pl.ds(1, self.n - 1)]
        pltpu.make_async_copy(arrived, arrived, self.sems.at[which]).wait()

    def wait_recv(self):
        self._wait(1)

    def wait_send(self):
        self._wait(0)


class Reduce:
    def __init__(self, n_g, n_z, part, grs, zsrc, zrs, zag, gag, sems):
        self.n_g, self.n_z, self.part, self.zsrc = n_g, n_z, part, zsrc
        self.height, self.width = zsrc.shape[1:]
        self.across = part.shape[2] // self.width
        self.grs = Exchange("outer", n_g, grs, sems.at[0])
        self.zrs = Exchange("dp", n_z, zrs, sems.at[1])
        self.zag = Exchange("dp", n_z, zag, sems.at[2])
        self.gag = Exchange("outer", n_g, gag, sems.at[3])

    def place(self, piece):
        down, right = piece // self.across * self.height, piece % self.across * self.width
        return slice(down, down + self.height), slice(right, right + self.width)

    def scatter_outer(self):
        self.grs.start(lambda to: self.part.at[to])

    def scatter_dp(self):
        self.grs.wait_recv()
        self.grs.slots[0] = self.part[self.grs.me()]
        total = self.grs.get(0)
        for source in range(1, self.n_g):
            total = total + self.grs.get(source)
        for piece in range(self.n_z):
            self.zsrc[piece] = total[self.place(piece)]
        self.zrs.start(lambda to: self.zsrc.at[to])

    def gather_dp(self):
        self.zrs.wait_recv()
        self.zrs.slots[0] = self.zsrc[self.zrs.me()]
        total = self.zrs.get(0)
        for source in range(1, self.n_z):
            total = total + self.zrs.get(source)
        self.zag.slots[0] = total
        self.zag.start(lambda to: self.zag.slots.at[0])

    def gather_outer(self):
        self.zag.wait_recv()
        for piece in range(self.n_z):
            self.gag.slots[(0, *self.place(piece))] = self.zag.get(piece)
        self.gag.start(lambda to: self.gag.slots.at[0])

    def finish(self):
        self.gag.wait_recv()
        return [self.gag.get(source) for source in range(self.n_g)]

    def drain(self):
        for exchange in (self.grs, self.zrs, self.zag, self.gag):
            exchange.wait_send()


def kernel(
    sizes,
    acts, dy, err, q,
    out, q_out,
    held, dyv, dyall, qv, wsrc, wex, vex, gex, pfull, prow, elim,
    part_p, grs_p, zsrc_p, zrs_p, zag_p, gag_p,
    part_u, grs_u, zsrc_u, zrs_u, zag_u, gag_u,
    loc, ring_send, ring_recv, dyz_sems, dyx_sems, wex_sems, vex_sems, gram_sems, p_sems, u_sems,
):
    n_g, n_z, n_x = sizes
    z, x = lax.axis_index("dp"), lax.axis_index("tensor")
    tok, cols = acts.shape
    rows = dy.shape[1]
    rows_z = rows // n_z
    rank = q.shape[0]
    quarter, part = tok // n_x, tok // CHUNKS
    steps = n_z // 2

    loads = [
        pltpu.make_async_copy(src, dst, loc.at[i])
        for i, (src, dst) in enumerate(((acts, held.at[0]), (q, qv), (err, out), (dy, dyv)))
    ]
    for load in loads:
        load.start()
    my_tokens = pl.ds(pl.multiple_of(x * quarter, quarter), quarter)
    own_dy = pltpu.make_async_copy(
        dy.at[my_tokens, pl.ds(pl.multiple_of(z * rows_z, rows_z), rows_z)], dyall.at[0, my_tokens, :], loc.at[4]
    )
    own_dy.start()

    barrier = pltpu.get_barrier_semaphore()
    for axis, n in (("dp", n_z), ("tensor", n_x), ("outer", n_g)):
        def greet(d, carry, axis=axis, n=n):
            to = lax.rem(lax.axis_index(axis) + d, n)
            pl.semaphore_signal(barrier, inc=1, device_id={axis: to}, device_id_type=MESH)
            return carry

        lax.fori_loop(1, n, greet, 0)
    pl.semaphore_wait(barrier, n_z + n_x + n_g - 3)

    def chunk(slot, c):
        return held.at[slot, pl.ds(c * part, part), :]

    def ring_copy(direction, s, c):
        here, there = (s, s + 1) if direction == 0 else ((n_z - s) % n_z, n_z - s - 1)
        to = lax.rem(z + (1 if direction == 0 else n_z - 1), n_z)
        return pltpu.make_async_remote_copy(
            src_ref=acts.at[pl.ds(c * part, part), :] if s == 0 else chunk(here, c),
            dst_ref=chunk(there, c),
            send_sem=ring_send.at[direction, s, c],
            recv_sem=ring_recv.at[direction, s, c],
            device_id={"dp": to},
            device_id_type=MESH,
        )

    def sends(s, c):
        return [ring_copy(direction, s, c) for direction in range(2) if s < steps - 1 or (c < RIGHT) == (direction == 0)]

    for c in range(CHUNKS):
        for copy in sends(0, c):
            copy.start()

    def send_dy(d, carry):
        to = lax.rem(z + d, n_z)
        pltpu.make_async_remote_copy(
            src_ref=dy.at[my_tokens, pl.ds(pl.multiple_of(to * rows_z, rows_z), rows_z)],
            dst_ref=dyall.at[d, my_tokens, :],
            send_sem=dyz_sems.at[0],
            recv_sem=dyz_sems.at[1],
            device_id={"dp": to},
            device_id_type=MESH,
        ).start()
        return carry

    lax.fori_loop(1, n_z, send_dy, 0)

    def wait_dyz(which):
        arrived = dyall.at[pl.ds(1, n_z - 1), pl.ds(0, quarter), :]
        pltpu.make_async_copy(arrived, arrived, dyz_sems.at[which]).wait()

    def send_dyx(piece):
        if piece == 0:
            wait_dyz(1)
            own_dy.wait()

        def send(d, carry):
            mine = dyall.at[pl.ds(piece * steps, steps), my_tokens, :]
            pltpu.make_async_remote_copy(
                src_ref=mine,
                dst_ref=mine,
                send_sem=dyx_sems.at[0, piece],
                recv_sem=dyx_sems.at[1, piece],
                device_id={"tensor": lax.rem(x + d, n_x)},
                device_id_type=MESH,
            ).start()
            return carry

        lax.fori_loop(1, n_x, send, 0)

    def wait_dyx(which):
        for piece in range(2):
            arrived = dyall.at[pl.ds(piece * steps, steps), pl.ds(0, quarter * (n_x - 1)), :]
            pltpu.make_async_copy(arrived, arrived, dyx_sems.at[which, piece]).wait()

    p_sum = Reduce(n_g, n_z, part_p, grs_p, zsrc_p, zrs_p, zag_p, gag_p, p_sems)
    u_sum = Reduce(n_g, n_z, part_u, grs_u, zsrc_u, zrs_u, zag_u, gag_u, u_sems)
    w_exchange = Exchange("tensor", n_x, wex, wex_sems)
    v_exchange = Exchange("tensor", n_x, vex, vex_sems)
    gram_exchange = Exchange("outer", n_g, gex, gram_sems)
    wide = rows // n_g
    my_rows = pl.ds(pl.multiple_of(z * rows_z, rows_z), rows_z)

    def start_w():
        for load in loads[:3]:
            load.wait()
        qt = qv[...]
        wsrc[:, :, :tok] = dot3(qt, held[0], NT).reshape(n_x, rank // n_x, tok)
        wsrc[:, :, tok:] = dot(qt, out[...], NT, HIGH).reshape(n_x, rank // n_x, rows_z)
        w_exchange.start(lambda to: wsrc.at[to])

    def start_p():
        w_exchange.wait_recv()
        loads[3].wait()
        wex[0] = wsrc[x]
        total = w_exchange.get(0)
        for source in range(1, n_x):
            total = total + w_exchange.get(source)
        pt = dot3(total[:, :tok], dyv[...], NN)
        for group in range(n_g):
            part_p[group] = pt[:, group * wide : (group + 1) * wide]
        mine = z * rows_z
        part_p[mine // wide, :, pl.ds(pl.multiple_of(lax.rem(mine, wide), 128), rows_z)] += total[:, tok:]
        p_sum.scatter_outer()

    def gather_p():
        pt = jnp.concatenate(p_sum.finish(), axis=1) * (1.0 / n_g)
        pfull[...] = pt
        vex[0, :, :tok] = dot3(pt, dyv[...], NT)
        vex[0, :, tok : tok + rows_z] = pfull[:, my_rows]
        vex[0, :, tok + rows_z :] = gag_p[0] * (1.0 / n_g)
        v_exchange.start(lambda to: vex.at[0])

    def start_u():
        v_exchange.wait_recv()
        vr = jnp.concatenate([v_exchange.get(source) for source in range(n_x)], axis=0)
        own_rows, some_rows = vr[:, tok : tok + rows_z], vr[:, tok + rows_z :]
        prow[...] = own_rows
        ut = dot3(vr[:, :tok], held[0], NN) + dot(own_rows, out[...], NN, HIGH)
        part_u[...] = ut.reshape(n_g, rank // n_g, cols)
        u_sum.scatter_outer()
        gram = dot(some_rows, some_rows, NT, HIGH)
        gex[0] = jnp.concatenate([gram, jnp.zeros_like(gram)], axis=1)
        gram_exchange.start(lambda to: gex.at[0])

    def start_gram():
        gram_exchange.wait_recv()
        gram = gram_exchange.get(0)
        for source in range(1, n_g):
            gram = gram + gram_exchange.get(source)
        row = lax.broadcasted_iota(jnp.int32, (rank, rank), 0)
        col = lax.broadcasted_iota(jnp.int32, (rank, rank), 1)
        elim[:, :rank] = (row == col).astype(F32)
        elim[:, rank:] = gram[:, :rank]

    def eliminate(first, last):
        row = lax.broadcasted_iota(jnp.int32, (rank, 2 * rank), 0)
        lane = lax.broadcasted_iota(jnp.int32, (rank, 2 * rank), 1)
        lane1 = lax.broadcasted_iota(jnp.int32, (1, 2 * rank), 1)

        def column(j, carry):
            whole = elim[...]
            pivot_row = elim[pl.ds(j, 1), :]
            pivot = jnp.sum(jnp.where(lane1 == rank + j, pivot_row, 0.0), axis=1, keepdims=True)
            scale = 1.0 / jnp.sqrt(pivot)
            pivot_row = pivot_row * scale
            factor = jnp.sum(jnp.where(lane == rank + j, whole, 0.0), axis=1, keepdims=True) * scale
            elim[...] = jnp.where(row > j, whole - factor * pivot_row, jnp.where(row == j, pivot_row, whole))
            return carry

        lax.fori_loop(first, last, column, 0)

    def finish_u():
        q_out[...] = jnp.concatenate(u_sum.finish(), axis=0)

    def correct():
        inverse = elim[:, :rank]
        qt = dot(inverse, q_out[...], NN, HIGH) * (1.0 / n_g)
        pt = dot(inverse, prow[...], NN, HIGH)
        q_out[...] = qt
        p_hi, q_hi = pt.astype(BF16), qt.astype(BF16)
        p_lo, q_lo = (pt - p_hi.astype(F32)).astype(BF16), (qt - q_hi.astype(F32)).astype(BF16)
        left = jnp.concatenate([p_hi, p_hi, p_lo], axis=0)
        right = jnp.concatenate([q_hi, q_lo, q_hi], axis=0)
        out[...] -= dot(left, right, TN)

    def add(slot):
        out[...] += dot(dyall[slot], held[slot], TN)

    def add_piece(slot, first, count):
        some = pl.ds(first * part, count * part)
        out[...] += dot(dyall[slot, some, :], held[slot, some, :], TN)

    last = CHUNKS * steps - 1
    work = [
        (5, p_sum.scatter_dp),
        (8, lambda: send_dyx(0)),
        (9, p_sum.gather_dp),
        (10, lambda: send_dyx(1)),
        (12, p_sum.gather_outer),
        (14, gather_p),
        (16, start_u),
        (18, u_sum.scatter_dp),
        (19, lambda: wait_dyx(1)),
        (19, start_gram),
        (20, lambda: eliminate(0, rank // 2)),
        (21, u_sum.gather_dp),
        (22, lambda: eliminate(rank // 2, rank)),
        (24, u_sum.gather_outer),
        (26, finish_u),
        (28, correct),
    ]
    order = [0] + [slot for d in range(1, steps) for slot in (d, n_z - d)]
    for i, slot in enumerate(order):
        arrived = CHUNKS * min(slot, n_z - slot) + CHUNKS - 1
        work.append((max(19 + i // 2, arrived), functools.partial(add, slot)))
    work.sort(key=lambda entry: entry[0])

    start_w()
    start_p()
    for t in range(CHUNKS, last + 1):
        s, c = t // CHUNKS, t % CHUNKS
        for copy in sends(s - 1, c):
            copy.wait_recv()
        for copy in sends(s, c):
            copy.start()
        for at, do in work:
            if at == t or (t == last and at > last):
                do()
    for c in range(max(RIGHT, CHUNKS - RIGHT)):
        for first, count in ((c, RIGHT), (RIGHT + c, CHUNKS)):
            if first < count:
                for copy in sends(steps - 1, first):
                    copy.wait_recv()
                add_piece(steps, first, 1)
    for s in range(steps):
        for c in range(CHUNKS):
            for copy in sends(s, c):
                copy.wait_send()
    wait_dyz(0)
    wait_dyx(0)
    w_exchange.wait_send()
    v_exchange.wait_send()
    gram_exchange.wait_send()
    p_sum.drain()
    u_sum.drain()


def local(sizes, acts, out_grads, error, q_warm):
    n_g, n_z, n_x = sizes
    tok, cols = acts.shape
    rows = out_grads.shape[1]
    rows_z = rows // n_z
    rank = q_warm.shape[1]

    def reduce_scratch(height, width):
        across = min(n_z, width // 128)
        piece = pltpu.VMEM((n_z, height * across // n_z, width // across), F32)
        whole = pltpu.VMEM((n_g, height, width), F32)
        return [whole, whole, piece, piece, piece, whole]

    anywhere = pl.BlockSpec(memory_space=pl.ANY)
    in_vmem = pl.BlockSpec(memory_space=pltpu.VMEM)
    dma = pltpu.SemaphoreType.DMA
    new_error, q_next = pl.pallas_call(
        functools.partial(kernel, sizes),
        out_shape=(
            pltpu.VMEM((rows_z, cols), F32),
            pltpu.VMEM((rank, cols), F32),
        ),
        in_specs=[anywhere] * 4,
        out_specs=(in_vmem, in_vmem),
        scratch_shapes=[
            pltpu.VMEM((n_z, tok, cols), BF16),
            pltpu.VMEM((tok, rows), BF16),
            pltpu.VMEM((n_z, tok, rows_z), BF16),
            pltpu.VMEM((rank, cols), F32),
            pltpu.VMEM((n_x, rank // n_x, tok + rows_z), F32),
            pltpu.VMEM((n_x, rank // n_x, tok + rows_z), F32),
            pltpu.VMEM((n_x, rank // n_x, tok + rows_z + rows // n_g), F32),
            pltpu.VMEM((n_g, rank, 2 * rank), F32),
            pltpu.VMEM((rank // n_x, rows), F32),
            pltpu.VMEM((rank, rows_z), F32),
            pltpu.VMEM((rank, 2 * rank), F32),
            *reduce_scratch(rank // n_x, rows // n_g),
            *reduce_scratch(rank // n_g, cols),
            dma((5,)),
            dma((2, n_z // 2, CHUNKS)),
            dma((2, n_z // 2, CHUNKS)),
            dma((2,)),
            dma((2, 2)),
            dma((2,)),
            dma((2,)),
            dma((2,)),
            dma((4, 2)),
            dma((4, 2)),
        ],
        compiler_params=pltpu.CompilerParams(
            collective_id=0, has_side_effects=True, vmem_limit_bytes=VMEM * 1024 * 1024
        ),
        cost_estimate=pl.CostEstimate(
            flops=2 * rows_z * cols * tok * n_z, bytes_accessed=2 * tok * (cols + rows) + 8 * rows_z * cols, transcendentals=0
        ),
        name="powersgd_step",
    )(*(pltpu.with_memory_space_constraint(a, pltpu.HBM) for a in (acts, out_grads, error[0], q_warm.T)))
    return new_error[None], q_next.T


def solution(mesh):
    sizes = (mesh.shape["outer"], mesh.shape["dp"], mesh.shape["tensor"])
    in_specs = (
        P(("outer", "dp"), "tensor"),
        P(("outer", "dp"), None),
        P("outer", "dp", "tensor"),
        P("tensor", None),
    )
    out_specs = (P("outer", "dp", "tensor"), P("tensor", None))
    return jax.shard_map(
        functools.partial(local, sizes), mesh=mesh, in_specs=in_specs, out_specs=out_specs, check_vma=False
    )
```

```python
import functools

import jax
import jax.numpy as jnp
from jax import lax
from jax.experimental import pallas as pl
from jax.experimental.pallas import tpu as pltpu
from jax.sharding import PartitionSpec as P

MESH = pl.DeviceIdType.MESH
VMEM = 62
CHUNKS = 4
RIGHT = 2
F32 = jnp.float32
BF16 = jnp.bfloat16
HIGH = lax.Precision.HIGHEST
NN = (((1,), (0,)), ((), ()))
NT = (((1,), (1,)), ((), ()))
TN = (((0,), (0,)), ((), ()))


def dot(a, b, dims, precision=None):
    return lax.dot_general(a, b, dims, precision=precision, preferred_element_type=F32)


def split3(a):
    hi = a.astype(BF16)
    rest = a - hi.astype(F32)
    mid = rest.astype(BF16)
    low = (rest - mid.astype(F32)).astype(BF16)
    return jnp.concatenate([hi, mid, low], axis=0)


def dot3(a, b, dims):
    k = a.shape[0]
    full = dot(split3(a), b, dims)
    return (full[2 * k :] + full[k : 2 * k]) + full[:k]


class Exchange:
    def __init__(self, axis, n, slots, sems):
        self.axis, self.n, self.slots, self.sems = axis, n, slots, sems

    def me(self):
        return lax.axis_index(self.axis)

    def get(self, source):
        return self.slots[lax.rem(self.me() + self.n - source, self.n)]

    def start(self, source):
        def send(d, carry):
            to = lax.rem(self.me() + d, self.n)
            pltpu.make_async_remote_copy(
                src_ref=source(to),
                dst_ref=self.slots.at[d],
                send_sem=self.sems.at[0],
                recv_sem=self.sems.at[1],
                device_id={self.axis: to},
                device_id_type=MESH,
            ).start()
            return carry

        lax.fori_loop(1, self.n, send, 0)

    def _wait(self, which):
        arrived = self.slots.at[pl.ds(1, self.n - 1)]
        pltpu.make_async_copy(arrived, arrived, self.sems.at[which]).wait()

    def wait_recv(self):
        self._wait(1)

    def wait_send(self):
        self._wait(0)


class Reduce:
    def __init__(self, n_g, n_z, part, grs, zsrc, zrs, zag, gag, sems):
        self.n_g, self.n_z, self.part, self.zsrc = n_g, n_z, part, zsrc
        self.height, self.width = zsrc.shape[1:]
        self.across = part.shape[2] // self.width
        self.grs = Exchange("outer", n_g, grs, sems.at[0])
        self.zrs = Exchange("dp", n_z, zrs, sems.at[1])
        self.zag = Exchange("dp", n_z, zag, sems.at[2])
        self.gag = Exchange("outer", n_g, gag, sems.at[3])

    def place(self, piece):
        down, right = piece // self.across * self.height, piece % self.across * self.width
        return slice(down, down + self.height), slice(right, right + self.width)

    def scatter_outer(self):
        self.grs.start(lambda to: self.part.at[to])

    def scatter_dp(self):
        self.grs.wait_recv()
        self.grs.slots[0] = self.part[self.grs.me()]
        total = self.grs.get(0)
        for source in range(1, self.n_g):
            total = total + self.grs.get(source)
        for piece in range(self.n_z):
            self.zsrc[piece] = total[self.place(piece)]
        self.zrs.start(lambda to: self.zsrc.at[to])

    def gather_dp(self):
        self.zrs.wait_recv()
        self.zrs.slots[0] = self.zsrc[self.zrs.me()]
        total = self.zrs.get(0)
        for source in range(1, self.n_z):
            total = total + self.zrs.get(source)
        self.zag.slots[0] = total
        self.zag.start(lambda to: self.zag.slots.at[0])

    def gather_outer(self):
        self.zag.wait_recv()
        for piece in range(self.n_z):
            self.gag.slots[(0, *self.place(piece))] = self.zag.get(piece)
        self.gag.start(lambda to: self.gag.slots.at[0])

    def finish(self):
        self.gag.wait_recv()
        return [self.gag.get(source) for source in range(self.n_g)]

    def drain(self):
        for exchange in (self.grs, self.zrs, self.zag, self.gag):
            exchange.wait_send()


def kernel(
    sizes,
    acts, dy, err, q,
    out, q_out,
    held, dyv, dyall, qv, wsrc, wex, vex, gex, pfull, prow, elim,
    part_p, grs_p, zsrc_p, zrs_p, zag_p, gag_p,
    part_u, grs_u, zsrc_u, zrs_u, zag_u, gag_u,
    loc, ring_send, ring_recv, dyz_sems, dyx_sems, wex_sems, vex_sems, gram_sems, p_sems, u_sems,
):
    n_g, n_z, n_x = sizes
    z, x = lax.axis_index("dp"), lax.axis_index("tensor")
    tok, cols = acts.shape
    rows = dy.shape[1]
    rows_z = rows // n_z
    rank = q.shape[0]
    quarter, part = tok // n_x, tok // CHUNKS
    steps = n_z // 2

    loads = [
        pltpu.make_async_copy(src, dst, loc.at[i])
        for i, (src, dst) in enumerate(((acts, held.at[0]), (q, qv), (err, out), (dy, dyv)))
    ]
    for load in loads:
        load.start()
    my_tokens = pl.ds(pl.multiple_of(x * quarter, quarter), quarter)
    own_dy = pltpu.make_async_copy(
        dy.at[my_tokens, pl.ds(pl.multiple_of(z * rows_z, rows_z), rows_z)], dyall.at[0, my_tokens, :], loc.at[4]
    )
    own_dy.start()

    barrier = pltpu.get_barrier_semaphore()
    for axis, n in (("dp", n_z), ("tensor", n_x), ("outer", n_g)):
        def greet(d, carry, axis=axis, n=n):
            to = lax.rem(lax.axis_index(axis) + d, n)
            pl.semaphore_signal(barrier, inc=1, device_id={axis: to}, device_id_type=MESH)
            return carry

        lax.fori_loop(1, n, greet, 0)
    pl.semaphore_wait(barrier, n_z + n_x + n_g - 3)

    def chunk(slot, c):
        return held.at[slot, pl.ds(c * part, part), :]

    def ring_copy(direction, s, c):
        here, there = (s, s + 1) if direction == 0 else ((n_z - s) % n_z, n_z - s - 1)
        to = lax.rem(z + (1 if direction == 0 else n_z - 1), n_z)
        return pltpu.make_async_remote_copy(
            src_ref=acts.at[pl.ds(c * part, part), :] if s == 0 else chunk(here, c),
            dst_ref=chunk(there, c),
            send_sem=ring_send.at[direction, s, c],
            recv_sem=ring_recv.at[direction, s, c],
            device_id={"dp": to},
            device_id_type=MESH,
        )

    def sends(s, c):
        return [ring_copy(direction, s, c) for direction in range(2) if s < steps - 1 or (c < RIGHT) == (direction == 0)]

    for c in range(CHUNKS):
        for copy in sends(0, c):
            copy.start()

    def send_dyz(d, carry):
        to = lax.rem(z + d, n_z)
        pltpu.make_async_remote_copy(
            src_ref=dy.at[my_tokens, pl.ds(pl.multiple_of(to * rows_z, rows_z), rows_z)],
            dst_ref=dyall.at[d, my_tokens, :],
            send_sem=dyz_sems.at[0],
            recv_sem=dyz_sems.at[1],
            device_id={"dp": to},
            device_id_type=MESH,
        ).start()
        return carry

    def start_dyz():
        lax.fori_loop(1, n_z, send_dyz, 0)

    def wait_dyz(which):
        arrived = dyall.at[pl.ds(1, n_z - 1), pl.ds(0, quarter), :]
        pltpu.make_async_copy(arrived, arrived, dyz_sems.at[which]).wait()

    def send_dyx(piece):
        if piece == 0:
            wait_dyz(1)
            own_dy.wait()

        def send(d, carry):
            mine = dyall.at[pl.ds(piece * steps, steps), my_tokens, :]
            pltpu.make_async_remote_copy(
                src_ref=mine,
                dst_ref=mine,
                send_sem=dyx_sems.at[0, piece],
                recv_sem=dyx_sems.at[1, piece],
                device_id={"tensor": lax.rem(x + d, n_x)},
                device_id_type=MESH,
            ).start()
            return carry

        lax.fori_loop(1, n_x, send, 0)

    def wait_dyx(which):
        for piece in range(2):
            arrived = dyall.at[pl.ds(piece * steps, steps), pl.ds(0, quarter * (n_x - 1)), :]
            pltpu.make_async_copy(arrived, arrived, dyx_sems.at[which, piece]).wait()

    p_sum = Reduce(n_g, n_z, part_p, grs_p, zsrc_p, zrs_p, zag_p, gag_p, p_sems)
    u_sum = Reduce(n_g, n_z, part_u, grs_u, zsrc_u, zrs_u, zag_u, gag_u, u_sems)
    w_exchange = Exchange("tensor", n_x, wex, wex_sems)
    v_exchange = Exchange("tensor", n_x, vex, vex_sems)
    gram_exchange = Exchange("outer", n_g, gex, gram_sems)
    wide = rows // n_g
    my_rows = pl.ds(pl.multiple_of(z * rows_z, rows_z), rows_z)

    def start_w():
        for load in loads[:3]:
            load.wait()
        qt = qv[...]
        wsrc[:, :, :tok] = dot3(qt, held[0], NT).reshape(n_x, rank // n_x, tok)
        wsrc[:, :, tok:] = dot(qt, out[...], NT, HIGH).reshape(n_x, rank // n_x, rows_z)
        w_exchange.start(lambda to: wsrc.at[to])

    def start_p():
        w_exchange.wait_recv()
        loads[3].wait()
        wex[0] = wsrc[x]
        total = w_exchange.get(0)
        for source in range(1, n_x):
            total = total + w_exchange.get(source)
        pt = dot3(total[:, :tok], dyv[...], NN)
        for group in range(n_g):
            part_p[group] = pt[:, group * wide : (group + 1) * wide]
        mine = z * rows_z
        part_p[mine // wide, :, pl.ds(pl.multiple_of(lax.rem(mine, wide), 128), rows_z)] += total[:, tok:]
        p_sum.scatter_outer()

    def gather_p():
        pt = jnp.concatenate(p_sum.finish(), axis=1) * (1.0 / n_g)
        pfull[...] = pt
        vex[0, :, :tok] = dot3(pt, dyv[...], NT)
        vex[0, :, tok : tok + rows_z] = pfull[:, my_rows]
        vex[0, :, tok + rows_z :] = gag_p[0] * (1.0 / n_g)
        v_exchange.start(lambda to: vex.at[0])

    def start_u():
        v_exchange.wait_recv()
        vr = jnp.concatenate([v_exchange.get(source) for source in range(n_x)], axis=0)
        own_rows, some_rows = vr[:, tok : tok + rows_z], vr[:, tok + rows_z :]
        prow[...] = own_rows
        ut = dot3(vr[:, :tok], held[0], NN) + dot(own_rows, out[...], NN, HIGH)
        part_u[...] = ut.reshape(n_g, rank // n_g, cols)
        u_sum.scatter_outer()
        gram = dot(some_rows, some_rows, NT, HIGH)
        gex[0] = jnp.concatenate([gram, jnp.zeros_like(gram)], axis=1)
        gram_exchange.start(lambda to: gex.at[0])

    def start_gram():
        gram_exchange.wait_recv()
        gram = gram_exchange.get(0)
        for source in range(1, n_g):
            gram = gram + gram_exchange.get(source)
        row = lax.broadcasted_iota(jnp.int32, (rank, rank), 0)
        col = lax.broadcasted_iota(jnp.int32, (rank, rank), 1)
        elim[:, :rank] = (row == col).astype(F32)
        elim[:, rank:] = gram[:, :rank]

    def eliminate(first, last):
        row = lax.broadcasted_iota(jnp.int32, (rank, 2 * rank), 0)
        lane = lax.broadcasted_iota(jnp.int32, (rank, 2 * rank), 1)
        lane1 = lax.broadcasted_iota(jnp.int32, (1, 2 * rank), 1)

        def column(j, carry):
            whole = elim[...]
            pivot_row = elim[pl.ds(j, 1), :]
            pivot = jnp.sum(jnp.where(lane1 == rank + j, pivot_row, 0.0), axis=1, keepdims=True)
            scale = 1.0 / jnp.sqrt(pivot)
            pivot_row = pivot_row * scale
            factor = jnp.sum(jnp.where(lane == rank + j, whole, 0.0), axis=1, keepdims=True) * scale
            elim[...] = jnp.where(row > j, whole - factor * pivot_row, jnp.where(row == j, pivot_row, whole))
            return carry

        lax.fori_loop(first, last, column, 0)

    def finish_u():
        q_out[...] = jnp.concatenate(u_sum.finish(), axis=0)

    def correct():
        inverse = elim[:, :rank]
        qt = dot(inverse, q_out[...], NN, HIGH) * (1.0 / n_g)
        pt = dot(inverse, prow[...], NN, HIGH)
        q_out[...] = qt
        p_hi, q_hi = pt.astype(BF16), qt.astype(BF16)
        p_lo, q_lo = (pt - p_hi.astype(F32)).astype(BF16), (qt - q_hi.astype(F32)).astype(BF16)
        left = jnp.concatenate([p_hi, p_hi, p_lo], axis=0)
        right = jnp.concatenate([q_hi, q_lo, q_hi], axis=0)
        out[...] -= dot(left, right, TN)

    def add(slot):
        out[...] += dot(dyall[slot], held[slot], TN)

    def add_piece(slot, first, count):
        some = pl.ds(first * part, count * part)
        out[...] += dot(dyall[slot, some, :], held[slot, some, :], TN)

    last = CHUNKS * steps - 1
    work = [
        (5, start_p),
        (7, p_sum.scatter_dp),
        (10, p_sum.gather_dp),
        (10, start_dyz),
        (13, p_sum.gather_outer),
        (13, gather_p),
        (13, start_u),
        (15, u_sum.scatter_dp),
        (15, start_gram),
        (16, lambda: send_dyx(0)),
        (16, lambda: eliminate(0, rank // 2)),
        (17, lambda: send_dyx(1)),
        (19, u_sum.gather_dp),
        (21, lambda: eliminate(rank // 2, rank)),
        (22, u_sum.gather_outer),
        (23, lambda: wait_dyx(1)),
        (25, finish_u),
        (27, correct),
    ]
    order = [0] + [slot for d in range(1, steps) for slot in (d, n_z - d)]
    for i, slot in enumerate(order):
        arrived = CHUNKS * min(slot, n_z - slot) + CHUNKS - 1
        work.append((max(23 + i // 2, arrived), functools.partial(add, slot)))
    work.sort(key=lambda entry: entry[0])

    start_w()
    for t in range(CHUNKS, last + 1):
        s, c = t // CHUNKS, t % CHUNKS
        for copy in sends(s - 1, c):
            copy.wait_recv()
        for copy in sends(s, c):
            copy.start()
        for at, do in work:
            if at == t or (t == last and at > last):
                do()
    for c in range(max(RIGHT, CHUNKS - RIGHT)):
        for first, count in ((c, RIGHT), (RIGHT + c, CHUNKS)):
            if first < count:
                for copy in sends(steps - 1, first):
                    copy.wait_recv()
                add_piece(steps, first, 1)
    for s in range(steps):
        for c in range(CHUNKS):
            for copy in sends(s, c):
                copy.wait_send()
    wait_dyz(0)
    wait_dyx(0)
    w_exchange.wait_send()
    v_exchange.wait_send()
    gram_exchange.wait_send()
    p_sum.drain()
    u_sum.drain()


def local(sizes, acts, out_grads, error, q_warm):
    n_g, n_z, n_x = sizes
    tok, cols = acts.shape
    rows = out_grads.shape[1]
    rows_z = rows // n_z
    rank = q_warm.shape[1]

    def reduce_scratch(height, width):
        across = min(n_z, width // 128)
        piece = pltpu.VMEM((n_z, height * across // n_z, width // across), F32)
        whole = pltpu.VMEM((n_g, height, width), F32)
        return [whole, whole, piece, piece, piece, whole]

    anywhere = pl.BlockSpec(memory_space=pl.ANY)
    in_vmem = pl.BlockSpec(memory_space=pltpu.VMEM)
    dma = pltpu.SemaphoreType.DMA
    new_error, q_next = pl.pallas_call(
        functools.partial(kernel, sizes),
        out_shape=(
            pltpu.VMEM((rows_z, cols), F32),
            pltpu.VMEM((rank, cols), F32),
        ),
        in_specs=[anywhere] * 4,
        out_specs=(in_vmem, in_vmem),
        scratch_shapes=[
            pltpu.VMEM((n_z, tok, cols), BF16),
            pltpu.VMEM((tok, rows), BF16),
            pltpu.VMEM((n_z, tok, rows_z), BF16),
            pltpu.VMEM((rank, cols), F32),
            pltpu.VMEM((n_x, rank // n_x, tok + rows_z), F32),
            pltpu.VMEM((n_x, rank // n_x, tok + rows_z), F32),
            pltpu.VMEM((n_x, rank // n_x, tok + rows_z + rows // n_g), F32),
            pltpu.VMEM((n_g, rank, 2 * rank), F32),
            pltpu.VMEM((rank // n_x, rows), F32),
            pltpu.VMEM((rank, rows_z), F32),
            pltpu.VMEM((rank, 2 * rank), F32),
            *reduce_scratch(rank // n_x, rows // n_g),
            *reduce_scratch(rank // n_g, cols),
            dma((5,)),
            dma((2, n_z // 2, CHUNKS)),
            dma((2, n_z // 2, CHUNKS)),
            dma((2,)),
            dma((2, 2)),
            dma((2,)),
            dma((2,)),
            dma((2,)),
            dma((4, 2)),
            dma((4, 2)),
        ],
        compiler_params=pltpu.CompilerParams(
            collective_id=0, has_side_effects=True, vmem_limit_bytes=VMEM * 1024 * 1024
        ),
        cost_estimate=pl.CostEstimate(
            flops=2 * rows_z * cols * tok * n_z, bytes_accessed=2 * tok * (cols + rows) + 8 * rows_z * cols, transcendentals=0
        ),
        name="powersgd_step",
    )(*(pltpu.with_memory_space_constraint(a, pltpu.HBM) for a in (acts, out_grads, error[0], q_warm.T)))
    return new_error[None], q_next.T


def solution(mesh):
    sizes = (mesh.shape["outer"], mesh.shape["dp"], mesh.shape["tensor"])
    in_specs = (
        P(("outer", "dp"), "tensor"),
        P(("outer", "dp"), None),
        P("outer", "dp", "tensor"),
        P("tensor", None),
    )
    out_specs = (P("outer", "dp", "tensor"), P("tensor", None))
    return jax.shard_map(
        functools.partial(local, sizes), mesh=mesh, in_specs=in_specs, out_specs=out_specs, check_vma=False
    )
```

```python
import functools

import jax
import jax.numpy as jnp
from jax import lax
from jax.experimental import pallas as pl
from jax.experimental.pallas import tpu as pltpu
from jax.sharding import PartitionSpec as P

MESH = pl.DeviceIdType.MESH
CHUNKS = 4
RIGHT = 2
F32 = jnp.float32
BF16 = jnp.bfloat16
HIGH = lax.Precision.HIGHEST
NN = (((1,), (0,)), ((), ()))
NT = (((1,), (1,)), ((), ()))
TN = (((0,), (0,)), ((), ()))


def dot(a, b, dims, precision=None):
    return lax.dot_general(a, b, dims, precision=precision, preferred_element_type=F32)


def split3(a):
    hi = a.astype(BF16)
    rest = a - hi.astype(F32)
    mid = rest.astype(BF16)
    low = (rest - mid.astype(F32)).astype(BF16)
    return jnp.concatenate([hi, mid, low], axis=0)


def dot3(a, b, dims):
    k = a.shape[0]
    full = dot(split3(a), b, dims)
    return (full[2 * k :] + full[k : 2 * k]) + full[:k]


class Exchange:
    def __init__(self, axis, n, slots, sems, stride=1, shift=0):
        self.axis, self.n, self.slots, self.sems, self.stride, self.shift = axis, n, slots, sems, stride, shift

    def index(self, place):
        return lax.rem(place + self.shift, self.n * self.stride) // self.stride

    def me(self):
        return self.index(lax.axis_index(self.axis))

    def get(self, source):
        return self.slots[lax.rem(self.me() + self.n - source, self.n)]

    def start(self, source):
        def send(d, carry):
            to = lax.rem(lax.axis_index(self.axis) + d * self.stride, self.n * self.stride)
            pltpu.make_async_remote_copy(
                src_ref=source(self.index(to)),
                dst_ref=self.slots.at[d],
                send_sem=self.sems.at[0],
                recv_sem=self.sems.at[1],
                device_id={self.axis: to},
                device_id_type=MESH,
            ).start()
            return carry

        lax.fori_loop(1, self.n, send, 0)

    def _wait(self, which):
        arrived = self.slots.at[pl.ds(1, self.n - 1)]
        pltpu.make_async_copy(arrived, arrived, self.sems.at[which]).wait()

    def wait_recv(self):
        self._wait(1)

    def wait_send(self):
        self._wait(0)


class Reduce:
    def __init__(self, n_g, n_z, part, grs, zsrc, zrs, zag, gag, sems):
        self.n_g, self.n_z, self.part, self.zsrc = n_g, n_z, part, zsrc
        self.height, self.width = zsrc.shape[1:]
        self.across = part.shape[2] // self.width
        self.grs = Exchange("outer", n_g, grs, sems.at[0])
        self.zrs = Exchange("dp", n_z, zrs, sems.at[1])
        self.zag = Exchange("dp", n_z, zag, sems.at[2])
        self.gag = Exchange("outer", n_g, gag, sems.at[3])

    def place(self, piece):
        down, right = piece // self.across * self.height, piece % self.across * self.width
        return slice(down, down + self.height), slice(right, right + self.width)

    def scatter_outer(self):
        self.grs.start(lambda to: self.part.at[to])

    def scatter_dp(self):
        self.grs.wait_recv()
        self.grs.slots[0] = self.part[self.grs.me()]
        total = self.grs.get(0)
        for source in range(1, self.n_g):
            total = total + self.grs.get(source)
        for piece in range(self.n_z):
            self.zsrc[piece] = total[self.place(piece)]
        self.zrs.start(lambda to: self.zsrc.at[to])

    def gather_dp(self):
        self.zrs.wait_recv()
        self.zrs.slots[0] = self.zsrc[self.zrs.me()]
        total = self.zrs.get(0)
        for source in range(1, self.n_z):
            total = total + self.zrs.get(source)
        self.zag.slots[0] = total
        self.zag.start(lambda to: self.zag.slots.at[0])

    def gather_outer(self):
        self.zag.wait_recv()
        for piece in range(self.n_z):
            self.gag.slots[(0, *self.place(piece))] = self.zag.get(piece)
        self.gag.start(lambda to: self.gag.slots.at[0])

    def finish(self):
        self.gag.wait_recv()
        return [self.gag.get(source) for source in range(self.n_g)]

    def drain(self):
        for exchange in (self.grs, self.zrs, self.zag, self.gag):
            exchange.wait_send()


class Pair:
    def __init__(self, to, slot, sems):
        self.to, self.slot, self.sems = to, slot, sems

    def start(self, source):
        pltpu.make_async_remote_copy(
            src_ref=source,
            dst_ref=self.slot,
            send_sem=self.sems.at[0],
            recv_sem=self.sems.at[1],
            device_id={"dp": self.to},
            device_id_type=MESH,
        ).start()

    def wait_recv(self):
        pltpu.make_async_copy(self.slot, self.slot, self.sems.at[1]).wait()

    def wait_send(self):
        pltpu.make_async_copy(self.slot, self.slot, self.sems.at[0]).wait()


class PairReduce(Reduce):
    def __init__(self, n_g, n_z, part, grs, zsrc, zpair, zmid, zrs, zag, zback, gag, sems):
        self.n_g, self.half, self.part, self.zsrc, self.zmid = n_g, n_z // 2, part, zsrc, zmid
        self.height, self.width = zsrc.shape[2:]
        self.across = part.shape[2] // self.width
        shift = lax.rem(lax.axis_index("outer"), 2)
        z = lax.axis_index("dp")
        self.parity = lax.rem(z + shift, 2)
        partner = lax.rem(z + n_z + 1 - 2 * self.parity, n_z)
        self.grs = Exchange("outer", n_g, grs, sems.at[0])
        self.pair = Pair(partner, zpair, sems.at[1])
        self.zrs = Exchange("dp", self.half, zrs, sems.at[2], 2, shift)
        self.zag = Exchange("dp", self.half, zag, sems.at[3], 2, shift)
        self.back = Pair(partner, zback, sems.at[4])
        self.gag = Exchange("outer", n_g, gag, sems.at[5])

    def place(self, piece):
        down, right = piece // self.across * self.height, piece % self.across * self.width
        return slice(down, down + self.height), slice(right, right + self.width)

    def scatter_outer(self):
        self.grs.start(lambda to: self.part.at[to])

    def swap_dp(self):
        self.grs.wait_recv()
        self.grs.slots[0] = self.part[self.grs.me()]
        total = self.grs.get(0)
        for source in range(1, self.n_g):
            total = total + self.grs.get(source)
        for piece in range(2 * self.half):
            self.zsrc[piece % 2, piece // 2] = total[self.place(piece)]
        self.pair.start(self.zsrc.at[1 - self.parity])

    def scatter_dp(self):
        self.pair.wait_recv()
        self.zmid[...] = self.zsrc[self.parity] + self.pair.slot[...]
        self.zrs.start(lambda to: self.zmid.at[to])

    def gather_dp(self):
        self.zrs.wait_recv()
        self.zrs.slots[0] = self.zmid[self.zrs.me()]
        total = self.zrs.get(0)
        for source in range(1, self.half):
            total = total + self.zrs.get(source)
        self.zag.slots[0] = total
        self.zag.start(lambda to: self.zag.slots.at[0])

    def swap_back(self):
        self.zag.wait_recv()
        self.back.start(self.zag.slots)

    def gather_outer(self):
        self.back.wait_recv()
        mine = self.zag.me()
        for piece in range(2 * self.half):
            slot = lax.rem(mine + self.half - piece // 2, self.half)
            block = jnp.where(self.parity == piece % 2, self.zag.slots[slot], self.back.slot[slot])
            self.gag.slots[(0, *self.place(piece))] = block
        self.gag.start(lambda to: self.gag.slots.at[0])

    def finish(self):
        self.gag.wait_recv()
        return [self.gag.get(source) for source in range(self.n_g)]

    def drain(self):
        for exchange in (self.grs, self.pair, self.zrs, self.zag, self.back, self.gag):
            exchange.wait_send()


def kernel(
    sizes,
    acts, dy, err, q,
    out, q_out,
    held, dyv, dyall, qv, wsrc, wex, vex, gex, pfull, prow, elim,
    part_p, grs_p, zsrc_p, zrs_p, zag_p, gag_p,
    part_u, grs_u, zsrc_u, zpair_u, zmid_u, zrs_u, zag_u, zback_u, gag_u,
    loc, ring_send, ring_recv, dyz_sems, dyx_sems, wex_sems, vex_sems, gram_sems, p_sems, u_sems,
):
    n_g, n_z, n_x = sizes
    z, x = lax.axis_index("dp"), lax.axis_index("tensor")
    tok, cols = acts.shape
    rows = dy.shape[1]
    rows_z = rows // n_z
    rank = q.shape[0]
    quarter, part = tok // n_x, tok // CHUNKS
    steps = n_z // 2

    loads = [
        pltpu.make_async_copy(src, dst, loc.at[i])
        for i, (src, dst) in enumerate(((acts, held.at[0]), (q, qv), (err, out), (dy, dyv)))
    ]
    for load in loads:
        load.start()
    my_tokens = pl.ds(pl.multiple_of(x * quarter, quarter), quarter)
    own_dy = pltpu.make_async_copy(
        dy.at[my_tokens, pl.ds(pl.multiple_of(z * rows_z, rows_z), rows_z)], dyall.at[0, my_tokens, :], loc.at[4]
    )
    own_dy.start()

    barrier = pltpu.get_barrier_semaphore()
    for axis, n in (("dp", n_z), ("tensor", n_x), ("outer", n_g)):
        def greet(d, carry, axis=axis, n=n):
            to = lax.rem(lax.axis_index(axis) + d, n)
            pl.semaphore_signal(barrier, inc=1, device_id={axis: to}, device_id_type=MESH)
            return carry

        lax.fori_loop(1, n, greet, 0)
    pl.semaphore_wait(barrier, n_z + n_x + n_g - 3)

    def chunk(slot, c):
        return held.at[slot, pl.ds(c * part, part), :]

    def ring_copy(direction, s, c):
        here, there = (s, s + 1) if direction == 0 else ((n_z - s) % n_z, n_z - s - 1)
        to = lax.rem(z + (1 if direction == 0 else n_z - 1), n_z)
        return pltpu.make_async_remote_copy(
            src_ref=acts.at[pl.ds(c * part, part), :] if s == 0 else chunk(here, c),
            dst_ref=chunk(there, c),
            send_sem=ring_send.at[direction, s, c],
            recv_sem=ring_recv.at[direction, s, c],
            device_id={"dp": to},
            device_id_type=MESH,
        )

    def sends(s, c):
        return [ring_copy(direction, s, c) for direction in range(2) if s < steps - 1 or (c < RIGHT) == (direction == 0)]

    for c in range(CHUNKS):
        for copy in sends(0, c):
            copy.start()

    def send_dyz(d, carry):
        to = lax.rem(z + d, n_z)
        pltpu.make_async_remote_copy(
            src_ref=dy.at[my_tokens, pl.ds(pl.multiple_of(to * rows_z, rows_z), rows_z)],
            dst_ref=dyall.at[d, my_tokens, :],
            send_sem=dyz_sems.at[0],
            recv_sem=dyz_sems.at[1],
            device_id={"dp": to},
            device_id_type=MESH,
        ).start()
        return carry

    def start_dyz():
        lax.fori_loop(1, n_z, send_dyz, 0)

    def wait_dyz(which):
        arrived = dyall.at[pl.ds(1, n_z - 1), pl.ds(0, quarter), :]
        pltpu.make_async_copy(arrived, arrived, dyz_sems.at[which]).wait()

    def send_dyx(piece):
        if piece == 0:
            wait_dyz(1)
            own_dy.wait()

        def send(d, carry):
            mine = dyall.at[pl.ds(piece * steps, steps), my_tokens, :]
            pltpu.make_async_remote_copy(
                src_ref=mine,
                dst_ref=mine,
                send_sem=dyx_sems.at[0, piece],
                recv_sem=dyx_sems.at[1, piece],
                device_id={"tensor": lax.rem(x + d, n_x)},
                device_id_type=MESH,
            ).start()
            return carry

        lax.fori_loop(1, n_x, send, 0)

    def wait_dyx(which):
        for piece in range(2):
            arrived = dyall.at[pl.ds(piece * steps, steps), pl.ds(0, quarter * (n_x - 1)), :]
            pltpu.make_async_copy(arrived, arrived, dyx_sems.at[which, piece]).wait()

    p_sum = Reduce(n_g, n_z, part_p, grs_p, zsrc_p, zrs_p, zag_p, gag_p, p_sems)
    u_sum = PairReduce(n_g, n_z, part_u, grs_u, zsrc_u, zpair_u, zmid_u, zrs_u, zag_u, zback_u, gag_u, u_sems)
    w_exchange = Exchange("tensor", n_x, wex, wex_sems)
    v_exchange = Exchange("tensor", n_x, vex, vex_sems)
    gram_exchange = Exchange("outer", n_g, gex, gram_sems)
    wide = rows // n_g
    my_rows = pl.ds(pl.multiple_of(z * rows_z, rows_z), rows_z)

    def start_w():
        for load in loads[:3]:
            load.wait()
        qt = qv[...]
        wsrc[:, :, :tok] = dot3(qt, held[0], NT).reshape(n_x, rank // n_x, tok)
        wsrc[:, :, tok:] = dot(qt, out[...], NT, HIGH).reshape(n_x, rank // n_x, rows_z)
        w_exchange.start(lambda to: wsrc.at[to])

    def start_p():
        w_exchange.wait_recv()
        loads[3].wait()
        wex[0] = wsrc[x]
        total = w_exchange.get(0)
        for source in range(1, n_x):
            total = total + w_exchange.get(source)
        pt = dot3(total[:, :tok], dyv[...], NN)
        for group in range(n_g):
            part_p[group] = pt[:, group * wide : (group + 1) * wide]
        mine = z * rows_z
        part_p[mine // wide, :, pl.ds(pl.multiple_of(lax.rem(mine, wide), 128), rows_z)] += total[:, tok:]
        p_sum.scatter_outer()

    def gather_p():
        pt = jnp.concatenate(p_sum.finish(), axis=1) * (1.0 / n_g)
        pfull[...] = pt
        vex[0, :, :tok] = dot3(pt, dyv[...], NT)
        vex[0, :, tok : tok + rows_z] = pfull[:, my_rows]
        vex[0, :, tok + rows_z :] = gag_p[0] * (1.0 / n_g)
        v_exchange.start(lambda to: vex.at[0])

    def start_u():
        v_exchange.wait_recv()
        vr = jnp.concatenate([v_exchange.get(source) for source in range(n_x)], axis=0)
        own_rows, some_rows = vr[:, tok : tok + rows_z], vr[:, tok + rows_z :]
        prow[...] = own_rows
        ut = dot3(vr[:, :tok], held[0], NN) + dot(own_rows, out[...], NN, HIGH)
        part_u[...] = ut.reshape(n_g, rank // n_g, cols)
        u_sum.scatter_outer()
        gram = dot(some_rows, some_rows, NT, HIGH)
        gex[0] = jnp.concatenate([gram, jnp.zeros_like(gram)], axis=1)
        gram_exchange.start(lambda to: gex.at[0])

    def start_gram():
        gram_exchange.wait_recv()
        gram = gram_exchange.get(0)
        for source in range(1, n_g):
            gram = gram + gram_exchange.get(source)
        row = lax.broadcasted_iota(jnp.int32, (rank, rank), 0)
        col = lax.broadcasted_iota(jnp.int32, (rank, rank), 1)
        elim[:, :rank] = (row == col).astype(F32)
        elim[:, rank:] = gram[:, :rank]

    def eliminate(first, last):
        row = lax.broadcasted_iota(jnp.int32, (rank, 2 * rank), 0)
        lane = lax.broadcasted_iota(jnp.int32, (rank, 2 * rank), 1)
        lane1 = lax.broadcasted_iota(jnp.int32, (1, 2 * rank), 1)

        def column(j, carry):
            whole = elim[...]
            pivot_row = elim[pl.ds(j, 1), :]
            pivot = jnp.sum(jnp.where(lane1 == rank + j, pivot_row, 0.0), axis=1, keepdims=True)
            scale = 1.0 / jnp.sqrt(pivot)
            pivot_row = pivot_row * scale
            factor = jnp.sum(jnp.where(lane == rank + j, whole, 0.0), axis=1, keepdims=True) * scale
            elim[...] = jnp.where(row > j, whole - factor * pivot_row, jnp.where(row == j, pivot_row, whole))
            return carry

        lax.fori_loop(first, last, column, 0)

    def finish_u():
        q_out[...] = jnp.concatenate(u_sum.finish(), axis=0)

    def correct():
        inverse = elim[:, :rank]
        qt = dot(inverse, q_out[...], NN, HIGH) * (1.0 / n_g)
        pt = dot(inverse, prow[...], NN, HIGH)
        q_out[...] = qt
        p_hi, q_hi = pt.astype(BF16), qt.astype(BF16)
        p_lo, q_lo = (pt - p_hi.astype(F32)).astype(BF16), (qt - q_hi.astype(F32)).astype(BF16)
        left = jnp.concatenate([p_hi, p_hi, p_lo], axis=0)
        right = jnp.concatenate([q_hi, q_lo, q_hi], axis=0)
        out[...] -= dot(left, right, TN)

    def add(slot):
        out[...] += dot(dyall[slot], held[slot], TN)

    def add_piece(slot, first, count):
        some = pl.ds(first * part, count * part)
        out[...] += dot(dyall[slot, some, :], held[slot, some, :], TN)

    last = CHUNKS * steps - 1
    work = [
        (5, start_p),
        (7, p_sum.scatter_dp),
        (10, p_sum.gather_dp),
        (10, start_dyz),
        (13, p_sum.gather_outer),
        (13, gather_p),
        (13, start_u),
        (15, u_sum.swap_dp),
        (15, start_gram),
        (16, lambda: send_dyx(0)),
        (16, lambda: eliminate(0, rank // 2)),
        (17, lambda: send_dyx(1)),
        (18, u_sum.scatter_dp),
        (20, u_sum.gather_dp),
        (21, lambda: eliminate(rank // 2, rank)),
        (23, lambda: wait_dyx(1)),
        (23, u_sum.swap_back),
        (26, u_sum.gather_outer),
        (28, finish_u),
        (29, correct),
    ]
    order = [0] + [slot for d in range(1, steps) for slot in (d, n_z - d)]
    for i, slot in enumerate(order):
        arrived = CHUNKS * min(slot, n_z - slot) + CHUNKS - 1
        work.append((max(23 + i // 2, arrived), functools.partial(add, slot)))
    work.sort(key=lambda entry: entry[0])

    start_w()
    for t in range(CHUNKS, last + 1):
        s, c = t // CHUNKS, t % CHUNKS
        for copy in sends(s - 1, c):
            copy.wait_recv()
        for copy in sends(s, c):
            copy.start()
        for at, do in work:
            if at == t or (t == last and at > last):
                do()
    for c in range(max(RIGHT, CHUNKS - RIGHT)):
        for first, count in ((c, RIGHT), (RIGHT + c, CHUNKS)):
            if first < count:
                for copy in sends(steps - 1, first):
                    copy.wait_recv()
                add_piece(steps, first, 1)
    for s in range(steps):
        for c in range(CHUNKS):
            for copy in sends(s, c):
                copy.wait_send()
    wait_dyz(0)
    wait_dyx(0)
    w_exchange.wait_send()
    v_exchange.wait_send()
    gram_exchange.wait_send()
    p_sum.drain()
    u_sum.drain()


def store(new_error, q_next, error_out, q_out, sems):
    copies = [
        pltpu.make_async_copy(new_error, error_out, sems.at[0]),
        pltpu.make_async_copy(q_next, q_out, sems.at[1]),
    ]
    for copy in copies:
        copy.start()
    for copy in copies:
        copy.wait()


def local(sizes, acts, out_grads, error, q_warm):
    n_g, n_z, n_x = sizes
    tok, cols = acts.shape
    rows = out_grads.shape[1]
    rows_z = rows // n_z
    rank = q_warm.shape[1]

    def reduce_scratch(height, width, paired):
        across = min(n_z, width // 128)
        piece = (height * across // n_z, width // across)
        whole = pltpu.VMEM((n_g, height, width), F32)
        pieces, half = pltpu.VMEM((n_z, *piece), F32), pltpu.VMEM((n_z // 2, *piece), F32)
        if paired:
            return [whole, whole, pltpu.VMEM((2, n_z // 2, *piece), F32), *[half] * 5, whole]
        return [whole, whole, *[pieces] * 3, whole]

    anywhere = pl.BlockSpec(memory_space=pl.ANY)
    in_vmem = pl.BlockSpec(memory_space=pltpu.VMEM)
    dma = pltpu.SemaphoreType.DMA
    new_error, q_next = pl.pallas_call(
        functools.partial(kernel, sizes),
        out_shape=(
            pltpu.VMEM((rows_z, cols), F32),
            pltpu.VMEM((rank, cols), F32),
        ),
        in_specs=[anywhere] * 4,
        out_specs=(in_vmem, in_vmem),
        scratch_shapes=[
            pltpu.VMEM((n_z, tok, cols), BF16),
            pltpu.VMEM((tok, rows), BF16),
            pltpu.VMEM((n_z, tok, rows_z), BF16),
            pltpu.VMEM((rank, cols), F32),
            pltpu.VMEM((n_x, rank // n_x, tok + rows_z), F32),
            pltpu.VMEM((n_x, rank // n_x, tok + rows_z), F32),
            pltpu.VMEM((n_x, rank // n_x, tok + rows_z + rows // n_g), F32),
            pltpu.VMEM((n_g, rank, 2 * rank), F32),
            pltpu.VMEM((rank // n_x, rows), F32),
            pltpu.VMEM((rank, rows_z), F32),
            pltpu.VMEM((rank, 2 * rank), F32),
            *reduce_scratch(rank // n_x, rows // n_g, False),
            *reduce_scratch(rank // n_g, cols, True),
            dma((5,)),
            dma((2, n_z // 2, CHUNKS)),
            dma((2, n_z // 2, CHUNKS)),
            dma((2,)),
            dma((2, 2)),
            dma((2,)),
            dma((2,)),
            dma((2,)),
            dma((4, 2)),
            dma((6, 2)),
        ],
        compiler_params=pltpu.CompilerParams(
            collective_id=0, has_side_effects=True, vmem_limit_bytes=48 * 1024 * 1024
        ),
        cost_estimate=pl.CostEstimate(
            flops=2 * rows_z * cols * tok * n_z, bytes_accessed=2 * tok * (cols + rows) + 8 * rows_z * cols, transcendentals=0
        ),
        name="powersgd_step",
    )(*(pltpu.with_memory_space_constraint(a, pltpu.HBM) for a in (acts, out_grads, error[0], q_warm.T)))
    new_error, q_next = pl.pallas_call(
        store,
        out_shape=(
            jax.ShapeDtypeStruct(new_error.shape, F32),
            jax.ShapeDtypeStruct(q_next.shape, F32),
        ),
        in_specs=[in_vmem] * 2,
        out_specs=(anywhere, anywhere),
        scratch_shapes=[dma((2,))],
        name="store_results",
    )(*(pltpu.with_memory_space_constraint(a, pltpu.VMEM) for a in (new_error, q_next)))
    return new_error[None], q_next.T


def solution(mesh):
    sizes = (mesh.shape["outer"], mesh.shape["dp"], mesh.shape["tensor"])
    in_specs = (
        P(("outer", "dp"), "tensor"),
        P(("outer", "dp"), None),
        P("outer", "dp", "tensor"),
        P("tensor", None),
    )
    out_specs = (P("outer", "dp", "tensor"), P("tensor", None))
    return jax.shard_map(
        functools.partial(local, sizes), mesh=mesh, in_specs=in_specs, out_specs=out_specs, check_vma=False
    )
```

```python
import functools

import jax
import jax.numpy as jnp
from jax import lax
from jax.experimental import pallas as pl
from jax.experimental.pallas import tpu as pltpu
from jax.sharding import PartitionSpec as P

MESH = pl.DeviceIdType.MESH
CHUNKS = 4
RIGHT = 2
F32 = jnp.float32
BF16 = jnp.bfloat16
HIGH = lax.Precision.HIGHEST
NN = (((1,), (0,)), ((), ()))
NT = (((1,), (1,)), ((), ()))
TN = (((0,), (0,)), ((), ()))


def dot(a, b, dims, precision=None):
    return lax.dot_general(a, b, dims, precision=precision, preferred_element_type=F32)


def split3(a):
    hi = a.astype(BF16)
    rest = a - hi.astype(F32)
    mid = rest.astype(BF16)
    low = (rest - mid.astype(F32)).astype(BF16)
    return jnp.concatenate([hi, mid, low], axis=0)


def dot3(a, b, dims):
    k = a.shape[0]
    full = dot(split3(a), b, dims)
    return (full[2 * k :] + full[k : 2 * k]) + full[:k]


class Exchange:
    def __init__(self, axis, n, slots, sems, stride=1, shift=0):
        self.axis, self.n, self.slots, self.sems, self.stride, self.shift = axis, n, slots, sems, stride, shift

    def index(self, place):
        return lax.rem(place + self.shift, self.n * self.stride) // self.stride

    def me(self):
        return self.index(lax.axis_index(self.axis))

    def get(self, source):
        return self.slots[lax.rem(self.me() + self.n - source, self.n)]

    def start(self, source):
        def send(d, carry):
            to = lax.rem(lax.axis_index(self.axis) + d * self.stride, self.n * self.stride)
            pltpu.make_async_remote_copy(
                src_ref=source(self.index(to)),
                dst_ref=self.slots.at[d],
                send_sem=self.sems.at[0],
                recv_sem=self.sems.at[1],
                device_id={self.axis: to},
                device_id_type=MESH,
            ).start()
            return carry

        lax.fori_loop(1, self.n, send, 0)

    def _wait(self, which):
        arrived = self.slots.at[pl.ds(1, self.n - 1)]
        pltpu.make_async_copy(arrived, arrived, self.sems.at[which]).wait()

    def wait_recv(self):
        self._wait(1)

    def wait_send(self):
        self._wait(0)


class Reduce:
    def __init__(self, n_g, n_z, part, grs, zsrc, zrs, zag, gag, sems):
        self.n_g, self.n_z, self.part, self.zsrc = n_g, n_z, part, zsrc
        self.height, self.width = zsrc.shape[1:]
        self.across = part.shape[2] // self.width
        self.grs = Exchange("outer", n_g, grs, sems.at[0])
        self.zrs = Exchange("dp", n_z, zrs, sems.at[1])
        self.zag = Exchange("dp", n_z, zag, sems.at[2])
        self.gag = Exchange("outer", n_g, gag, sems.at[3])

    def place(self, piece):
        down, right = piece // self.across * self.height, piece % self.across * self.width
        return slice(down, down + self.height), slice(right, right + self.width)

    def scatter_outer(self):
        self.grs.start(lambda to: self.part.at[to])

    def scatter_dp(self):
        self.grs.wait_recv()
        self.grs.slots[0] = self.part[self.grs.me()]
        total = self.grs.get(0)
        for source in range(1, self.n_g):
            total = total + self.grs.get(source)
        for piece in range(self.n_z):
            self.zsrc[piece] = total[self.place(piece)]
        self.zrs.start(lambda to: self.zsrc.at[to])

    def gather_dp(self):
        self.zrs.wait_recv()
        self.zrs.slots[0] = self.zsrc[self.zrs.me()]
        total = self.zrs.get(0)
        for source in range(1, self.n_z):
            total = total + self.zrs.get(source)
        self.zag.slots[0] = total
        self.zag.start(lambda to: self.zag.slots.at[0])

    def gather_outer(self):
        self.zag.wait_recv()
        for piece in range(self.n_z):
            self.gag.slots[(0, *self.place(piece))] = self.zag.get(piece)
        self.gag.start(lambda to: self.gag.slots.at[0])

    def finish(self):
        self.gag.wait_recv()
        return [self.gag.get(source) for source in range(self.n_g)]

    def drain(self):
        for exchange in (self.grs, self.zrs, self.zag, self.gag):
            exchange.wait_send()


class Pair:
    def __init__(self, to, slot, sems):
        self.to, self.slot, self.sems = to, slot, sems

    def start(self, source):
        pltpu.make_async_remote_copy(
            src_ref=source,
            dst_ref=self.slot,
            send_sem=self.sems.at[0],
            recv_sem=self.sems.at[1],
            device_id={"dp": self.to},
            device_id_type=MESH,
        ).start()

    def wait_recv(self):
        pltpu.make_async_copy(self.slot, self.slot, self.sems.at[1]).wait()

    def wait_send(self):
        pltpu.make_async_copy(self.slot, self.slot, self.sems.at[0]).wait()


class PairReduce(Reduce):
    def __init__(self, n_g, n_z, part, grs, zsrc, zpair, zmid, zrs, zag, zback, gag, sems):
        self.n_g, self.half, self.part, self.zsrc, self.zmid = n_g, n_z // 2, part, zsrc, zmid
        self.height, self.width = zsrc.shape[2:]
        self.across = part.shape[2] // self.width
        shift = lax.rem(lax.axis_index("outer"), 2)
        z = lax.axis_index("dp")
        self.parity = lax.rem(z + shift, 2)
        partner = lax.rem(z + n_z + 1 - 2 * self.parity, n_z)
        self.grs = Exchange("outer", n_g, grs, sems.at[0])
        self.pair = Pair(partner, zpair.at[pl.ds(0, self.half)], sems.at[1])
        self.zrs = Exchange("dp", self.half, zrs, sems.at[2], 2, shift)
        self.zag = Exchange("dp", self.half, zag, sems.at[3], 2, shift)
        self.back = Pair(partner, zback.at[pl.ds(0, self.half)], sems.at[4])
        self.gag = Exchange("outer", n_g, gag, sems.at[5])

    def place(self, piece):
        down, right = piece // self.across * self.height, piece % self.across * self.width
        return slice(down, down + self.height), slice(right, right + self.width)

    def scatter_outer(self):
        self.grs.start(lambda to: self.part.at[to])

    def swap_dp(self):
        self.grs.wait_recv()
        self.grs.slots[0] = self.part[self.grs.me()]
        total = self.grs.get(0)
        for source in range(1, self.n_g):
            total = total + self.grs.get(source)
        for piece in range(2 * self.half):
            self.zsrc[piece % 2, piece // 2] = total[self.place(piece)]
        self.pair.start(self.zsrc.at[1 - self.parity])

    def scatter_dp(self):
        self.pair.wait_recv()
        for piece in range(self.half):
            self.zmid[piece] = self.zsrc[self.parity, piece] + self.pair.slot[piece]
        self.zrs.start(lambda to: self.zmid.at[to])

    def gather_dp(self):
        self.zrs.wait_recv()
        self.zrs.slots[0] = self.zmid[self.zrs.me()]
        total = self.zrs.get(0)
        for source in range(1, self.half):
            total = total + self.zrs.get(source)
        self.zag.slots[0] = total
        self.zag.start(lambda to: self.zag.slots.at[0])

    def swap_back(self):
        self.zag.wait_recv()
        self.back.start(self.zag.slots.at[pl.ds(0, self.half)])

    def gather_outer(self):
        self.back.wait_recv()
        mine = self.zag.me()
        for piece in range(2 * self.half):
            slot = lax.rem(mine + self.half - piece // 2, self.half)
            block = jnp.where(self.parity == piece % 2, self.zag.slots[slot], self.back.slot[slot])
            self.gag.slots[(0, *self.place(piece))] = block
        self.gag.start(lambda to: self.gag.slots.at[0])

    def finish(self):
        self.gag.wait_recv()
        return [self.gag.get(source) for source in range(self.n_g)]

    def drain(self):
        for exchange in (self.grs, self.pair, self.zrs, self.zag, self.back, self.gag):
            exchange.wait_send()


def kernel(
    sizes,
    acts, dy, err, q,
    out, q_out,
    held, dyv, dyall, qv, wsrc, wex, vex, gex, pfull, prow, elim,
    part_p, grs_p, zsrc_p, zrs_p, zag_p, gag_p,
    part_u, grs_u, zsrc_u, zpair_u, zmid_u, zrs_u, zag_u, zback_u, gag_u,
    loc, ring_send, ring_recv, dyz_sems, dyx_sems, wex_sems, vex_sems, gram_sems, p_sems, u_sems,
):
    n_g, n_z, n_x = sizes
    z, x = lax.axis_index("dp"), lax.axis_index("tensor")
    tok, cols = acts.shape
    rows = dy.shape[1]
    rows_z = rows // n_z
    rank = q.shape[0]
    quarter, part = tok // n_x, tok // CHUNKS
    steps = n_z // 2

    loads = [
        pltpu.make_async_copy(src, dst, loc.at[i])
        for i, (src, dst) in enumerate(((acts, held.at[0]), (q, qv), (err, out), (dy, dyv)))
    ]
    for load in loads:
        load.start()
    my_tokens = pl.ds(pl.multiple_of(x * quarter, quarter), quarter)
    own_dy = pltpu.make_async_copy(
        dy.at[my_tokens, pl.ds(pl.multiple_of(z * rows_z, rows_z), rows_z)], dyall.at[0, my_tokens, :], loc.at[4]
    )
    own_dy.start()

    barrier = pltpu.get_barrier_semaphore()
    for axis, n in (("dp", n_z), ("tensor", n_x), ("outer", n_g)):
        def greet(d, carry, axis=axis, n=n):
            to = lax.rem(lax.axis_index(axis) + d, n)
            pl.semaphore_signal(barrier, inc=1, device_id={axis: to}, device_id_type=MESH)
            return carry

        lax.fori_loop(1, n, greet, 0)
    pl.semaphore_wait(barrier, n_z + n_x + n_g - 3)

    def chunk(slot, c):
        return held.at[slot, pl.ds(c * part, part), :]

    def ring_copy(direction, s, c):
        here, there = (s, s + 1) if direction == 0 else ((n_z - s) % n_z, n_z - s - 1)
        to = lax.rem(z + (1 if direction == 0 else n_z - 1), n_z)
        return pltpu.make_async_remote_copy(
            src_ref=acts.at[pl.ds(c * part, part), :] if s == 0 else chunk(here, c),
            dst_ref=chunk(there, c),
            send_sem=ring_send.at[direction, s, c],
            recv_sem=ring_recv.at[direction, s, c],
            device_id={"dp": to},
            device_id_type=MESH,
        )

    def sends(s, c):
        return [ring_copy(direction, s, c) for direction in range(2) if s < steps - 1 or (c < RIGHT) == (direction == 0)]

    for c in range(CHUNKS):
        for copy in sends(0, c):
            copy.start()

    def send_dyz(d, carry):
        to = lax.rem(z + d, n_z)
        pltpu.make_async_remote_copy(
            src_ref=dy.at[my_tokens, pl.ds(pl.multiple_of(to * rows_z, rows_z), rows_z)],
            dst_ref=dyall.at[d, my_tokens, :],
            send_sem=dyz_sems.at[0],
            recv_sem=dyz_sems.at[1],
            device_id={"dp": to},
            device_id_type=MESH,
        ).start()
        return carry

    def start_dyz():
        lax.fori_loop(1, n_z, send_dyz, 0)

    def wait_dyz(which):
        arrived = dyall.at[pl.ds(1, n_z - 1), pl.ds(0, quarter), :]
        pltpu.make_async_copy(arrived, arrived, dyz_sems.at[which]).wait()

    def send_dyx(piece):
        if piece == 0:
            wait_dyz(1)
            own_dy.wait()

        def send(d, carry):
            mine = dyall.at[pl.ds(piece * steps, steps), my_tokens, :]
            pltpu.make_async_remote_copy(
                src_ref=mine,
                dst_ref=mine,
                send_sem=dyx_sems.at[0, piece],
                recv_sem=dyx_sems.at[1, piece],
                device_id={"tensor": lax.rem(x + d, n_x)},
                device_id_type=MESH,
            ).start()
            return carry

        lax.fori_loop(1, n_x, send, 0)

    def wait_dyx(which):
        for piece in range(2):
            arrived = dyall.at[pl.ds(piece * steps, steps), pl.ds(0, quarter * (n_x - 1)), :]
            pltpu.make_async_copy(arrived, arrived, dyx_sems.at[which, piece]).wait()

    p_sum = Reduce(n_g, n_z, part_p, grs_p, zsrc_p, zrs_p, zag_p, gag_p, p_sems)
    u_sum = PairReduce(n_g, n_z, part_u, grs_u, zsrc_u, zpair_u, zmid_u, zrs_u, zag_u, zback_u, gag_u, u_sems)
    w_exchange = Exchange("tensor", n_x, wex, wex_sems)
    v_exchange = Exchange("tensor", n_x, vex, vex_sems)
    gram_exchange = Exchange("outer", n_g, gex, gram_sems)
    wide = rows // n_g
    my_rows = pl.ds(pl.multiple_of(z * rows_z, rows_z), rows_z)

    def start_w():
        for load in loads[:3]:
            load.wait()
        qt = qv[...]
        wsrc[:, :, :tok] = dot3(qt, held[0], NT).reshape(n_x, rank // n_x, tok)
        wsrc[:, :, tok:] = dot(qt, out[...], NT, HIGH).reshape(n_x, rank // n_x, rows_z)
        w_exchange.start(lambda to: wsrc.at[to])

    def start_p():
        w_exchange.wait_recv()
        loads[3].wait()
        wex[0] = wsrc[x]
        total = w_exchange.get(0)
        for source in range(1, n_x):
            total = total + w_exchange.get(source)
        pt = dot3(total[:, :tok], dyv[...], NN)
        for group in range(n_g):
            part_p[group] = pt[:, group * wide : (group + 1) * wide]
        mine = z * rows_z
        part_p[mine // wide, :, pl.ds(pl.multiple_of(lax.rem(mine, wide), 128), rows_z)] += total[:, tok:]
        p_sum.scatter_outer()

    def gather_p():
        pt = jnp.concatenate(p_sum.finish(), axis=1) * (1.0 / n_g)
        pfull[...] = pt
        vex[0, :, :tok] = dot3(pt, dyv[...], NT)
        vex[0, :, tok : tok + rows_z] = pfull[:, my_rows]
        vex[0, :, tok + rows_z :] = gag_p[0] * (1.0 / n_g)
        v_exchange.start(lambda to: vex.at[0])

    def start_u():
        v_exchange.wait_recv()
        vr = jnp.concatenate([v_exchange.get(source) for source in range(n_x)], axis=0)
        own_rows, some_rows = vr[:, tok : tok + rows_z], vr[:, tok + rows_z :]
        prow[...] = own_rows
        ut = dot3(vr[:, :tok], held[0], NN) + dot(own_rows, out[...], NN, HIGH)
        part_u[...] = ut.reshape(n_g, rank // n_g, cols)
        u_sum.scatter_outer()
        gram = dot(some_rows, some_rows, NT, HIGH)
        gex[0] = jnp.concatenate([gram, jnp.zeros_like(gram)], axis=1)
        gram_exchange.start(lambda to: gex.at[0])

    def start_gram():
        gram_exchange.wait_recv()
        gram = gram_exchange.get(0)
        for source in range(1, n_g):
            gram = gram + gram_exchange.get(source)
        row = lax.broadcasted_iota(jnp.int32, (rank, rank), 0)
        col = lax.broadcasted_iota(jnp.int32, (rank, rank), 1)
        elim[:rank, :rank] = (row == col).astype(F32)
        elim[:rank, rank:] = gram[:, :rank]

    def eliminate(first, last):
        row = lax.broadcasted_iota(jnp.int32, (rank, 2 * rank), 0)
        lane = lax.broadcasted_iota(jnp.int32, (rank, 2 * rank), 1)
        lane1 = lax.broadcasted_iota(jnp.int32, (1, 2 * rank), 1)

        def column(j, carry):
            whole = elim[:rank]
            pivot_row = elim[pl.ds(j, 1), :]
            pivot = jnp.sum(jnp.where(lane1 == rank + j, pivot_row, 0.0), axis=1, keepdims=True)
            scale = 1.0 / jnp.sqrt(pivot)
            pivot_row = pivot_row * scale
            factor = jnp.sum(jnp.where(lane == rank + j, whole, 0.0), axis=1, keepdims=True) * scale
            elim[:rank] = jnp.where(row > j, whole - factor * pivot_row, jnp.where(row == j, pivot_row, whole))
            return carry

        lax.fori_loop(first, last, column, 0)

    def finish_u():
        q_out[...] = jnp.concatenate(u_sum.finish(), axis=0)

    def correct():
        inverse = elim[:rank, :rank]
        qt = dot(inverse, q_out[...], NN, HIGH) * (1.0 / n_g)
        pt = dot(inverse, prow[...], NN, HIGH)
        q_out[...] = qt
        p_hi, q_hi = pt.astype(BF16), qt.astype(BF16)
        p_lo, q_lo = (pt - p_hi.astype(F32)).astype(BF16), (qt - q_hi.astype(F32)).astype(BF16)
        left = jnp.concatenate([p_hi, p_hi, p_lo], axis=0)
        right = jnp.concatenate([q_hi, q_lo, q_hi], axis=0)
        out[...] -= dot(left, right, TN)

    def add(slot):
        out[...] += dot(dyall[slot], held[slot], TN)

    def add_piece(slot, first, count):
        some = pl.ds(first * part, count * part)
        out[...] += dot(dyall[slot, some, :], held[slot, some, :], TN)

    last = CHUNKS * steps - 1
    work = [
        (5, start_p),
        (7, p_sum.scatter_dp),
        (10, p_sum.gather_dp),
        (10, start_dyz),
        (13, p_sum.gather_outer),
        (13, gather_p),
        (13, start_u),
        (15, u_sum.swap_dp),
        (15, start_gram),
        (16, lambda: send_dyx(0)),
        (16, lambda: eliminate(0, rank // 2)),
        (17, lambda: send_dyx(1)),
        (18, u_sum.scatter_dp),
        (20, u_sum.gather_dp),
        (21, lambda: eliminate(rank // 2, rank)),
        (23, lambda: wait_dyx(1)),
        (23, u_sum.swap_back),
        (26, u_sum.gather_outer),
        (28, finish_u),
        (29, correct),
    ]
    order = [0] + [slot for d in range(1, steps) for slot in (d, n_z - d)]
    for i, slot in enumerate(order):
        arrived = CHUNKS * min(slot, n_z - slot) + CHUNKS - 1
        work.append((max(23 + i // 2, arrived), functools.partial(add, slot)))
    work.sort(key=lambda entry: entry[0])

    start_w()
    for t in range(CHUNKS, last + 1):
        s, c = t // CHUNKS, t % CHUNKS
        for copy in sends(s - 1, c):
            copy.wait_recv()
        for copy in sends(s, c):
            copy.start()
        for at, do in work:
            if at == t or (t == last and at > last):
                do()
    for c in range(max(RIGHT, CHUNKS - RIGHT)):
        for first, count in ((c, RIGHT), (RIGHT + c, CHUNKS)):
            if first < count:
                for copy in sends(steps - 1, first):
                    copy.wait_recv()
                add_piece(steps, first, 1)
    for s in range(steps):
        for c in range(CHUNKS):
            for copy in sends(s, c):
                copy.wait_send()
    wait_dyz(0)
    wait_dyx(0)
    w_exchange.wait_send()
    v_exchange.wait_send()
    gram_exchange.wait_send()
    p_sum.drain()
    u_sum.drain()


def store(new_error, q_next, error_out, q_out, sems):
    copies = [
        pltpu.make_async_copy(new_error, error_out, sems.at[0]),
        pltpu.make_async_copy(q_next, q_out, sems.at[1]),
    ]
    for copy in copies:
        copy.start()
    for copy in copies:
        copy.wait()


def local(sizes, acts, out_grads, error, q_warm):
    n_g, n_z, n_x = sizes
    tok, cols = acts.shape
    rows = out_grads.shape[1]
    rows_z = rows // n_z
    rank = q_warm.shape[1]

    def reduce_scratch(height, width, paired):
        across = min(n_z, width // 128)
        piece = (height * across // n_z, width // across)
        whole = pltpu.VMEM((n_g, height, width), F32)
        pieces, half = pltpu.VMEM((n_z + 1, *piece), F32), pltpu.VMEM((n_z // 2 + 1, *piece), F32)
        if paired:
            return [whole, whole, pltpu.VMEM((3, n_z // 2, *piece), F32), *[half] * 5, whole]
        return [whole, whole, *[pieces] * 3, whole]

    anywhere = pl.BlockSpec(memory_space=pl.ANY)
    in_vmem = pl.BlockSpec(memory_space=pltpu.VMEM)
    dma = pltpu.SemaphoreType.DMA
    new_error, q_next = pl.pallas_call(
        functools.partial(kernel, sizes),
        out_shape=(
            pltpu.VMEM((rows_z, cols), F32),
            pltpu.VMEM((rank, cols), F32),
        ),
        in_specs=[anywhere] * 4,
        out_specs=(in_vmem, in_vmem),
        scratch_shapes=[
            pltpu.VMEM((n_z, tok, cols), BF16),
            pltpu.VMEM((tok, rows), BF16),
            pltpu.VMEM((n_z, tok, rows_z), BF16),
            pltpu.VMEM((rank, cols), F32),
            pltpu.VMEM((n_x, rank // n_x, tok + rows_z), F32),
            pltpu.VMEM((n_x, rank // n_x, tok + rows_z), F32),
            pltpu.VMEM((n_x, rank // n_x, tok + rows_z + rows // n_g), F32),
            pltpu.VMEM((n_g, rank, 2 * rank), F32),
            pltpu.VMEM((rank // n_x, rows), F32),
            pltpu.VMEM((rank, rows_z), F32),
            pltpu.VMEM((rank + 8, 2 * rank), F32),
            *reduce_scratch(rank // n_x, rows // n_g, False),
            *reduce_scratch(rank // n_g, cols, True),
            dma((5,)),
            dma((2, n_z // 2, CHUNKS)),
            dma((2, n_z // 2, CHUNKS)),
            dma((2,)),
            dma((2, 2)),
            dma((2,)),
            dma((2,)),
            dma((2,)),
            dma((4, 2)),
            dma((6, 2)),
        ],
        compiler_params=pltpu.CompilerParams(
            collective_id=0, has_side_effects=True, vmem_limit_bytes=48 * 1024 * 1024
        ),
        cost_estimate=pl.CostEstimate(
            flops=2 * rows_z * cols * tok * n_z, bytes_accessed=2 * tok * (cols + rows) + 8 * rows_z * cols, transcendentals=0
        ),
        name="powersgd_step",
    )(*(pltpu.with_memory_space_constraint(a, pltpu.HBM) for a in (acts, out_grads, error[0], q_warm.T)))
    new_error, q_next = pl.pallas_call(
        store,
        out_shape=(
            jax.ShapeDtypeStruct(new_error.shape, F32),
            jax.ShapeDtypeStruct(q_next.shape, F32),
        ),
        in_specs=[in_vmem] * 2,
        out_specs=(anywhere, anywhere),
        scratch_shapes=[dma((2,))],
        name="store_results",
    )(*(pltpu.with_memory_space_constraint(a, pltpu.VMEM) for a in (new_error, q_next)))
    return new_error[None], q_next.T


def solution(mesh):
    sizes = (mesh.shape["outer"], mesh.shape["dp"], mesh.shape["tensor"])
    in_specs = (
        P(("outer", "dp"), "tensor"),
        P(("outer", "dp"), None),
        P("outer", "dp", "tensor"),
        P("tensor", None),
    )
    out_specs = (P("outer", "dp", "tensor"), P("tensor", None))
    return jax.shard_map(
        functools.partial(local, sizes), mesh=mesh, in_specs=in_specs, out_specs=out_specs, check_vma=False
    )
```

```python
import functools

import jax
import jax.numpy as jnp
from jax import lax
from jax.experimental import pallas as pl
from jax.experimental.pallas import tpu as pltpu
from jax.sharding import PartitionSpec as P

MESH = pl.DeviceIdType.MESH
CHUNKS = 4
RIGHT = 2
F32 = jnp.float32
BF16 = jnp.bfloat16
HIGH = lax.Precision.HIGHEST
NN = (((1,), (0,)), ((), ()))
NT = (((1,), (1,)), ((), ()))
TN = (((0,), (0,)), ((), ()))


def dot(a, b, dims, precision=None):
    return lax.dot_general(a, b, dims, precision=precision, preferred_element_type=F32)


def split3(a):
    hi = a.astype(BF16)
    rest = a - hi.astype(F32)
    mid = rest.astype(BF16)
    low = (rest - mid.astype(F32)).astype(BF16)
    return jnp.concatenate([hi, mid, low], axis=0)


def dot3(a, b, dims):
    k = a.shape[0]
    full = dot(split3(a), b, dims)
    return (full[2 * k :] + full[k : 2 * k]) + full[:k]


class Exchange:
    def __init__(self, axis, n, slots, sems, stride=1, shift=0):
        self.axis, self.n, self.slots, self.sems, self.stride, self.shift = axis, n, slots, sems, stride, shift

    def index(self, place):
        return lax.rem(place + self.shift, self.n * self.stride) // self.stride

    def me(self):
        return self.index(lax.axis_index(self.axis))

    def get(self, source):
        return self.slots[lax.rem(self.me() + self.n - source, self.n)]

    def start(self, source):
        def send(d, carry):
            to = lax.rem(lax.axis_index(self.axis) + d * self.stride, self.n * self.stride)
            pltpu.make_async_remote_copy(
                src_ref=source(self.index(to)),
                dst_ref=self.slots.at[d],
                send_sem=self.sems.at[0],
                recv_sem=self.sems.at[1],
                device_id={self.axis: to},
                device_id_type=MESH,
            ).start()
            return carry

        lax.fori_loop(1, self.n, send, 0)

    def _wait(self, which):
        arrived = self.slots.at[pl.ds(1, self.n - 1)]
        pltpu.make_async_copy(arrived, arrived, self.sems.at[which]).wait()

    def wait_recv(self):
        self._wait(1)

    def wait_send(self):
        self._wait(0)


class Reduce:
    def __init__(self, n_g, n_z, part, grs, zsrc, zrs, zag, gag, sems):
        self.n_g, self.n_z, self.part, self.zsrc = n_g, n_z, part, zsrc
        self.height, self.width = zsrc.shape[1:]
        self.across = part.shape[2] // self.width
        self.grs = Exchange("outer", n_g, grs, sems.at[0])
        self.zrs = Exchange("dp", n_z, zrs, sems.at[1])
        self.zag = Exchange("dp", n_z, zag, sems.at[2])
        self.gag = Exchange("outer", n_g, gag, sems.at[3])

    def place(self, piece):
        down, right = piece // self.across * self.height, piece % self.across * self.width
        return slice(down, down + self.height), slice(right, right + self.width)

    def scatter_outer(self):
        self.grs.start(lambda to: self.part.at[to])

    def scatter_dp(self):
        self.grs.wait_recv()
        self.grs.slots[0] = self.part[self.grs.me()]
        total = self.grs.get(0)
        for source in range(1, self.n_g):
            total = total + self.grs.get(source)
        for piece in range(self.n_z):
            self.zsrc[piece] = total[self.place(piece)]
        self.zrs.start(lambda to: self.zsrc.at[to])

    def gather_dp(self):
        self.zrs.wait_recv()
        self.zrs.slots[0] = self.zsrc[self.zrs.me()]
        total = self.zrs.get(0)
        for source in range(1, self.n_z):
            total = total + self.zrs.get(source)
        self.zag.slots[0] = total
        self.zag.start(lambda to: self.zag.slots.at[0])

    def gather_outer(self):
        self.zag.wait_recv()
        for piece in range(self.n_z):
            self.gag.slots[(0, *self.place(piece))] = self.zag.get(piece)
        self.gag.start(lambda to: self.gag.slots.at[0])

    def finish(self):
        self.gag.wait_recv()
        return [self.gag.get(source) for source in range(self.n_g)]

    def drain(self):
        for exchange in (self.grs, self.zrs, self.zag, self.gag):
            exchange.wait_send()


class Pair:
    def __init__(self, to, slot, sems):
        self.to, self.slot, self.sems = to, slot, sems

    def start(self, source):
        pltpu.make_async_remote_copy(
            src_ref=source,
            dst_ref=self.slot,
            send_sem=self.sems.at[0],
            recv_sem=self.sems.at[1],
            device_id={"dp": self.to},
            device_id_type=MESH,
        ).start()

    def wait_recv(self):
        pltpu.make_async_copy(self.slot, self.slot, self.sems.at[1]).wait()

    def wait_send(self):
        pltpu.make_async_copy(self.slot, self.slot, self.sems.at[0]).wait()


class PairReduce(Reduce):
    def __init__(self, n_g, n_z, part, grs, zsrc, zpair, zmid, zrs, zag, zback, gag, sems):
        self.n_g, self.half, self.part, self.zsrc, self.zmid = n_g, n_z // 2, part, zsrc, zmid
        self.height, self.width = zsrc.shape[2:]
        self.across = part.shape[2] // self.width
        shift = lax.rem(lax.axis_index("outer"), 2)
        z = lax.axis_index("dp")
        self.parity = lax.rem(z + shift, 2)
        partner = lax.rem(z + n_z + 1 - 2 * self.parity, n_z)
        self.grs = Exchange("outer", n_g, grs, sems.at[0])
        self.pair = Pair(partner, zpair.at[pl.ds(0, self.half)], sems.at[1])
        self.zrs = Exchange("dp", self.half, zrs, sems.at[2], 2, shift)
        self.zag = Exchange("dp", self.half, zag, sems.at[3], 2, shift)
        self.back = Pair(partner, zback.at[pl.ds(0, self.half)], sems.at[4])
        self.gag = Exchange("outer", n_g, gag, sems.at[5])

    def place(self, piece):
        down, right = piece // self.across * self.height, piece % self.across * self.width
        return slice(down, down + self.height), slice(right, right + self.width)

    def scatter_outer(self):
        self.grs.start(lambda to: self.part.at[to])

    def swap_dp(self):
        self.grs.wait_recv()
        self.grs.slots[0] = self.part[self.grs.me()]
        total = self.grs.get(0)
        for source in range(1, self.n_g):
            total = total + self.grs.get(source)
        for piece in range(2 * self.half):
            self.zsrc[piece % 2, piece // 2] = total[self.place(piece)]
        self.pair.start(self.zsrc.at[1 - self.parity])

    def scatter_dp(self):
        self.pair.wait_recv()
        for piece in range(self.half):
            self.zmid[piece] = self.zsrc[self.parity, piece] + self.pair.slot[piece]
        self.zrs.start(lambda to: self.zmid.at[to])

    def gather_dp(self):
        self.zrs.wait_recv()
        self.zrs.slots[0] = self.zmid[self.zrs.me()]
        total = self.zrs.get(0)
        for source in range(1, self.half):
            total = total + self.zrs.get(source)
        self.zag.slots[0] = total
        self.zag.start(lambda to: self.zag.slots.at[0])

    def swap_back(self):
        self.zag.wait_recv()
        self.back.start(self.zag.slots.at[pl.ds(0, self.half)])

    def gather_outer(self):
        self.back.wait_recv()
        mine = self.zag.me()
        for piece in range(2 * self.half):
            slot = lax.rem(mine + self.half - piece // 2, self.half)
            block = jnp.where(self.parity == piece % 2, self.zag.slots[slot], self.back.slot[slot])
            self.gag.slots[(0, *self.place(piece))] = block
        self.gag.start(lambda to: self.gag.slots.at[0])

    def finish(self):
        self.gag.wait_recv()
        return [self.gag.get(source) for source in range(self.n_g)]

    def drain(self):
        for exchange in (self.grs, self.pair, self.zrs, self.zag, self.back, self.gag):
            exchange.wait_send()


def kernel(
    sizes,
    acts, dy, err, q,
    out, q_out,
    held, dyv, dyall, qv, wsrc, wex, vex, gex, pfull, prow, elim,
    part_p, grs_p, zsrc_p, zrs_p, zag_p, gag_p,
    part_u, grs_u, zsrc_u, zpair_u, zmid_u, zrs_u, zag_u, zback_u, gag_u,
    loc, ring_send, ring_recv, dyz_sems, dyx_sems, wex_sems, vex_sems, gram_sems, p_sems, u_sems,
):
    n_g, n_z, n_x = sizes
    z, x = lax.axis_index("dp"), lax.axis_index("tensor")
    tok, cols = acts.shape
    rows = dy.shape[1]
    rows_z = rows // n_z
    rank = q.shape[0]
    quarter, part = tok // n_x, tok // CHUNKS
    steps = n_z // 2

    loads = [
        pltpu.make_async_copy(src, dst, loc.at[i])
        for i, (src, dst) in enumerate(((acts, held.at[0]), (q, qv), (err, out), (dy, dyv)))
    ]
    for load in loads:
        load.start()
    my_tokens = pl.ds(pl.multiple_of(x * quarter, quarter), quarter)
    own_dy = pltpu.make_async_copy(
        dy.at[my_tokens, pl.ds(pl.multiple_of(z * rows_z, rows_z), rows_z)], dyall.at[0, my_tokens, :], loc.at[4]
    )
    own_dy.start()

    barrier = pltpu.get_barrier_semaphore()
    for axis, n in (("dp", n_z), ("tensor", n_x), ("outer", n_g)):
        def greet(d, carry, axis=axis, n=n):
            to = lax.rem(lax.axis_index(axis) + d, n)
            pl.semaphore_signal(barrier, inc=1, device_id={axis: to}, device_id_type=MESH)
            return carry

        lax.fori_loop(1, n, greet, 0)
    pl.semaphore_wait(barrier, n_z + n_x + n_g - 3)

    def chunk(slot, c):
        return held.at[slot, pl.ds(c * part, part), :]

    def ring_copy(direction, s, c):
        here, there = (s, s + 1) if direction == 0 else ((n_z - s) % n_z, n_z - s - 1)
        to = lax.rem(z + (1 if direction == 0 else n_z - 1), n_z)
        return pltpu.make_async_remote_copy(
            src_ref=acts.at[pl.ds(c * part, part), :] if s == 0 else chunk(here, c),
            dst_ref=chunk(there, c),
            send_sem=ring_send.at[direction, s, c],
            recv_sem=ring_recv.at[direction, s, c],
            device_id={"dp": to},
            device_id_type=MESH,
        )

    def sends(s, c):
        return [ring_copy(direction, s, c) for direction in range(2) if s < steps - 1 or (c < RIGHT) == (direction == 0)]

    for c in range(CHUNKS):
        for copy in sends(0, c):
            copy.start()

    def send_dyz(d, carry):
        to = lax.rem(z + d, n_z)
        pltpu.make_async_remote_copy(
            src_ref=dy.at[my_tokens, pl.ds(pl.multiple_of(to * rows_z, rows_z), rows_z)],
            dst_ref=dyall.at[d, my_tokens, :],
            send_sem=dyz_sems.at[0],
            recv_sem=dyz_sems.at[1],
            device_id={"dp": to},
            device_id_type=MESH,
        ).start()
        return carry

    def start_dyz():
        lax.fori_loop(1, n_z, send_dyz, 0)

    def wait_dyz(which):
        arrived = dyall.at[pl.ds(1, n_z - 1), pl.ds(0, quarter), :]
        pltpu.make_async_copy(arrived, arrived, dyz_sems.at[which]).wait()

    def send_dyx(piece):
        if piece == 0:
            wait_dyz(1)
            own_dy.wait()

        def send(d, carry):
            mine = dyall.at[pl.ds(piece * steps, steps), my_tokens, :]
            pltpu.make_async_remote_copy(
                src_ref=mine,
                dst_ref=mine,
                send_sem=dyx_sems.at[0, piece],
                recv_sem=dyx_sems.at[1, piece],
                device_id={"tensor": lax.rem(x + d, n_x)},
                device_id_type=MESH,
            ).start()
            return carry

        lax.fori_loop(1, n_x, send, 0)

    def wait_dyx(which):
        for piece in range(2):
            arrived = dyall.at[pl.ds(piece * steps, steps), pl.ds(0, quarter * (n_x - 1)), :]
            pltpu.make_async_copy(arrived, arrived, dyx_sems.at[which, piece]).wait()

    p_sum = Reduce(n_g, n_z, part_p, grs_p, zsrc_p, zrs_p, zag_p, gag_p, p_sems)
    u_sum = PairReduce(n_g, n_z, part_u, grs_u, zsrc_u, zpair_u, zmid_u, zrs_u, zag_u, zback_u, gag_u, u_sems)
    w_exchange = Exchange("tensor", n_x, wex, wex_sems)
    v_exchange = Exchange("tensor", n_x, vex, vex_sems)
    gram_exchange = Exchange("outer", n_g, gex, gram_sems)
    wide = rows // n_g
    my_rows = pl.ds(pl.multiple_of(z * rows_z, rows_z), rows_z)

    def start_w():
        for load in loads[:3]:
            load.wait()
        qt = qv[...]
        wsrc[:, :, :tok] = dot3(qt, held[0], NT).reshape(n_x, rank // n_x, tok)
        wsrc[:, :, tok:] = dot(qt, out[...], NT, HIGH).reshape(n_x, rank // n_x, rows_z)
        w_exchange.start(lambda to: wsrc.at[to])

    def start_p():
        w_exchange.wait_recv()
        loads[3].wait()
        wex[0] = wsrc[x]
        total = w_exchange.get(0)
        for source in range(1, n_x):
            total = total + w_exchange.get(source)
        pt = dot3(total[:, :tok], dyv[...], NN)
        for group in range(n_g):
            part_p[group] = pt[:, group * wide : (group + 1) * wide]
        mine = z * rows_z
        part_p[mine // wide, :, pl.ds(pl.multiple_of(lax.rem(mine, wide), 128), rows_z)] += total[:, tok:]
        p_sum.scatter_outer()

    def gather_p():
        pt = jnp.concatenate(p_sum.finish(), axis=1) * (1.0 / n_g)
        pfull[...] = pt
        vex[0, :, :tok] = dot3(pt, dyv[...], NT)
        vex[0, :, tok : tok + rows_z] = pfull[:, my_rows]
        vex[0, :, tok + rows_z :] = gag_p[0] * (1.0 / n_g)
        v_exchange.start(lambda to: vex.at[0])

    def start_u():
        v_exchange.wait_recv()
        vr = jnp.concatenate([v_exchange.get(source) for source in range(n_x)], axis=0)
        own_rows, some_rows = vr[:, tok : tok + rows_z], vr[:, tok + rows_z :]
        prow[...] = own_rows
        ut = dot3(vr[:, :tok], held[0], NN) + dot(own_rows, out[...], NN, HIGH)
        part_u[...] = ut.reshape(n_g, rank // n_g, cols)
        u_sum.scatter_outer()
        gram = dot(some_rows, some_rows, NT, HIGH)
        gex[0] = jnp.concatenate([gram, jnp.zeros_like(gram)], axis=1)
        gram_exchange.start(lambda to: gex.at[0])

    def start_gram():
        gram_exchange.wait_recv()
        gram = gram_exchange.get(0)
        for source in range(1, n_g):
            gram = gram + gram_exchange.get(source)
        row = lax.broadcasted_iota(jnp.int32, (rank, rank), 0)
        col = lax.broadcasted_iota(jnp.int32, (rank, rank), 1)
        elim[:rank, :rank] = (row == col).astype(F32)
        elim[:rank, rank:] = gram[:, :rank]

    def eliminate(first, last):
        row = lax.broadcasted_iota(jnp.int32, (rank, 2 * rank), 0)
        lane = lax.broadcasted_iota(jnp.int32, (rank, 2 * rank), 1)
        lane1 = lax.broadcasted_iota(jnp.int32, (1, 2 * rank), 1)

        def column(j, carry):
            whole = elim[:rank]
            pivot_row = elim[pl.ds(j, 1), :]
            pivot = jnp.sum(jnp.where(lane1 == rank + j, pivot_row, 0.0), axis=1, keepdims=True)
            scale = 1.0 / jnp.sqrt(pivot)
            pivot_row = pivot_row * scale
            factor = jnp.sum(jnp.where(lane == rank + j, whole, 0.0), axis=1, keepdims=True) * scale
            elim[:rank] = jnp.where(row > j, whole - factor * pivot_row, jnp.where(row == j, pivot_row, whole))
            return carry

        lax.fori_loop(first, last, column, 0)

    def finish_u():
        q_out[...] = jnp.concatenate(u_sum.finish(), axis=0)

    def correct():
        inverse = elim[:rank, :rank]
        qt = dot(inverse, q_out[...], NN, HIGH) * (1.0 / n_g)
        pt = dot(inverse, prow[...], NN, HIGH)
        q_out[...] = qt
        p_hi, q_hi = pt.astype(BF16), qt.astype(BF16)
        p_lo, q_lo = (pt - p_hi.astype(F32)).astype(BF16), (qt - q_hi.astype(F32)).astype(BF16)
        left = jnp.concatenate([p_hi, p_hi, p_lo], axis=0)
        right = jnp.concatenate([q_hi, q_lo, q_hi], axis=0)
        out[...] -= dot(left, right, TN)

    def add(slot):
        out[...] += dot(dyall[slot], held[slot], TN)

    def add_piece(slot, first, count):
        some = pl.ds(first * part, count * part)
        out[...] += dot(dyall[slot, some, :], held[slot, some, :], TN)

    last = CHUNKS * steps - 1
    work = [
        (4, start_p),
        (6, p_sum.scatter_dp),
        (9, p_sum.gather_dp),
        (9, start_dyz),
        (13, p_sum.gather_outer),
        (13, gather_p),
        (13, start_u),
        (15, u_sum.swap_dp),
        (15, start_gram),
        (16, lambda: send_dyx(0)),
        (16, lambda: eliminate(0, rank // 2)),
        (17, lambda: send_dyx(1)),
        (18, u_sum.scatter_dp),
        (20, u_sum.gather_dp),
        (21, lambda: eliminate(rank // 2, rank)),
        (23, lambda: wait_dyx(1)),
        (23, u_sum.swap_back),
        (26, u_sum.gather_outer),
        (28, finish_u),
        (29, correct),
    ]
    order = [0] + [slot for d in range(1, steps) for slot in (d, n_z - d)]
    for i, slot in enumerate(order):
        arrived = CHUNKS * min(slot, n_z - slot) + CHUNKS - 1
        work.append((max(23 + i // 2, arrived), functools.partial(add, slot)))
    work.sort(key=lambda entry: entry[0])

    start_w()
    for t in range(CHUNKS, last + 1):
        s, c = t // CHUNKS, t % CHUNKS
        for copy in sends(s - 1, c):
            copy.wait_recv()
        for copy in sends(s, c):
            copy.start()
        for at, do in work:
            if at == t or (t == last and at > last):
                do()
    for c in range(max(RIGHT, CHUNKS - RIGHT)):
        for first, count in ((c, RIGHT), (RIGHT + c, CHUNKS)):
            if first < count:
                for copy in sends(steps - 1, first):
                    copy.wait_recv()
                add_piece(steps, first, 1)
    for s in range(steps):
        for c in range(CHUNKS):
            for copy in sends(s, c):
                copy.wait_send()
    wait_dyz(0)
    wait_dyx(0)
    w_exchange.wait_send()
    v_exchange.wait_send()
    gram_exchange.wait_send()
    p_sum.drain()
    u_sum.drain()


def store(new_error, q_next, error_out, q_out, sems):
    copies = [
        pltpu.make_async_copy(new_error, error_out, sems.at[0]),
        pltpu.make_async_copy(q_next, q_out, sems.at[1]),
    ]
    for copy in copies:
        copy.start()
    for copy in copies:
        copy.wait()


def local(sizes, acts, out_grads, error, q_warm):
    n_g, n_z, n_x = sizes
    tok, cols = acts.shape
    rows = out_grads.shape[1]
    rows_z = rows // n_z
    rank = q_warm.shape[1]

    def reduce_scratch(height, width, paired):
        across = min(n_z, width // 128)
        piece = (height * across // n_z, width // across)
        whole = pltpu.VMEM((n_g, height, width), F32)
        pieces, half = pltpu.VMEM((n_z + 1, *piece), F32), pltpu.VMEM((n_z // 2 + 1, *piece), F32)
        if paired:
            return [whole, whole, pltpu.VMEM((3, n_z // 2, *piece), F32), *[half] * 5, whole]
        return [whole, whole, *[pieces] * 3, whole]

    anywhere = pl.BlockSpec(memory_space=pl.ANY)
    in_vmem = pl.BlockSpec(memory_space=pltpu.VMEM)
    dma = pltpu.SemaphoreType.DMA
    new_error, q_next = pl.pallas_call(
        functools.partial(kernel, sizes),
        out_shape=(
            pltpu.VMEM((rows_z, cols), F32),
            pltpu.VMEM((rank, cols), F32),
        ),
        in_specs=[anywhere] * 4,
        out_specs=(in_vmem, in_vmem),
        scratch_shapes=[
            pltpu.VMEM((n_z, tok, cols), BF16),
            pltpu.VMEM((tok, rows), BF16),
            pltpu.VMEM((n_z, tok, rows_z), BF16),
            pltpu.VMEM((rank, cols), F32),
            pltpu.VMEM((n_x, rank // n_x, tok + rows_z), F32),
            pltpu.VMEM((n_x, rank // n_x, tok + rows_z), F32),
            pltpu.VMEM((n_x, rank // n_x, tok + rows_z + rows // n_g), F32),
            pltpu.VMEM((n_g, rank, 2 * rank), F32),
            pltpu.VMEM((rank // n_x, rows), F32),
            pltpu.VMEM((rank, rows_z), F32),
            pltpu.VMEM((rank + 8, 2 * rank), F32),
            *reduce_scratch(rank // n_x, rows // n_g, False),
            *reduce_scratch(rank // n_g, cols, True),
            dma((5,)),
            dma((2, n_z // 2, CHUNKS)),
            dma((2, n_z // 2, CHUNKS)),
            dma((2,)),
            dma((2, 2)),
            dma((2,)),
            dma((2,)),
            dma((2,)),
            dma((4, 2)),
            dma((6, 2)),
        ],
        compiler_params=pltpu.CompilerParams(
            collective_id=0, has_side_effects=True, vmem_limit_bytes=48 * 1024 * 1024
        ),
        cost_estimate=pl.CostEstimate(
            flops=2 * rows_z * cols * tok * n_z, bytes_accessed=2 * tok * (cols + rows) + 8 * rows_z * cols, transcendentals=0
        ),
        name="powersgd_step",
    )(*(pltpu.with_memory_space_constraint(a, pltpu.HBM) for a in (acts, out_grads, error[0], q_warm.T)))
    new_error, q_next = pl.pallas_call(
        store,
        out_shape=(
            jax.ShapeDtypeStruct(new_error.shape, F32),
            jax.ShapeDtypeStruct(q_next.shape, F32),
        ),
        in_specs=[in_vmem] * 2,
        out_specs=(anywhere, anywhere),
        scratch_shapes=[dma((2,))],
        name="store_results",
    )(*(pltpu.with_memory_space_constraint(a, pltpu.VMEM) for a in (new_error, q_next)))
    return new_error[None], q_next.T


def solution(mesh):
    sizes = (mesh.shape["outer"], mesh.shape["dp"], mesh.shape["tensor"])
    in_specs = (
        P(("outer", "dp"), "tensor"),
        P(("outer", "dp"), None),
        P("outer", "dp", "tensor"),
        P("tensor", None),
    )
    out_specs = (P("outer", "dp", "tensor"), P("tensor", None))
    return jax.shard_map(
        functools.partial(local, sizes), mesh=mesh, in_specs=in_specs, out_specs=out_specs, check_vma=False
    )
```

```python
import functools

import jax
import jax.numpy as jnp
from jax import lax
from jax.experimental import pallas as pl
from jax.experimental.pallas import tpu as pltpu
from jax.sharding import PartitionSpec as P

MESH = pl.DeviceIdType.MESH
CHUNKS = 4
RIGHT = 2
F32 = jnp.float32
BF16 = jnp.bfloat16
HIGH = lax.Precision.HIGHEST
NN = (((1,), (0,)), ((), ()))
NT = (((1,), (1,)), ((), ()))
TN = (((0,), (0,)), ((), ()))


def dot(a, b, dims, precision=None):
    return lax.dot_general(a, b, dims, precision=precision, preferred_element_type=F32)


def split3(a):
    hi = a.astype(BF16)
    rest = a - hi.astype(F32)
    mid = rest.astype(BF16)
    low = (rest - mid.astype(F32)).astype(BF16)
    return jnp.concatenate([hi, mid, low], axis=0)


def dot3(a, b, dims):
    k = a.shape[0]
    full = dot(split3(a), b, dims)
    return (full[2 * k :] + full[k : 2 * k]) + full[:k]


class Exchange:
    def __init__(self, axis, n, slots, sems, stride=1, shift=0):
        self.axis, self.n, self.slots, self.sems, self.stride, self.shift = axis, n, slots, sems, stride, shift

    def index(self, place):
        return lax.rem(place + self.shift, self.n * self.stride) // self.stride

    def me(self):
        return self.index(lax.axis_index(self.axis))

    def get(self, source):
        return self.slots[lax.rem(self.me() + self.n - source, self.n)]

    def start(self, source):
        def send(d, carry):
            to = lax.rem(lax.axis_index(self.axis) + d * self.stride, self.n * self.stride)
            pltpu.make_async_remote_copy(
                src_ref=source(self.index(to)),
                dst_ref=self.slots.at[d],
                send_sem=self.sems.at[0],
                recv_sem=self.sems.at[1],
                device_id={self.axis: to},
                device_id_type=MESH,
            ).start()
            return carry

        lax.fori_loop(1, self.n, send, 0)

    def _wait(self, which):
        arrived = self.slots.at[pl.ds(1, self.n - 1)]
        pltpu.make_async_copy(arrived, arrived, self.sems.at[which]).wait()

    def wait_recv(self):
        self._wait(1)

    def wait_send(self):
        self._wait(0)


class Reduce:
    def __init__(self, n_g, n_z, part, grs, zsrc, zrs, zag, gag, sems):
        self.n_g, self.n_z, self.part, self.zsrc = n_g, n_z, part, zsrc
        self.height, self.width = zsrc.shape[1:]
        self.across = part.shape[2] // self.width
        self.grs = Exchange("outer", n_g, grs, sems.at[0])
        self.zrs = Exchange("dp", n_z, zrs, sems.at[1])
        self.zag = Exchange("dp", n_z, zag, sems.at[2])
        self.gag = Exchange("outer", n_g, gag, sems.at[3])

    def place(self, piece):
        down, right = piece // self.across * self.height, piece % self.across * self.width
        return slice(down, down + self.height), slice(right, right + self.width)

    def scatter_outer(self):
        self.grs.start(lambda to: self.part.at[to])

    def scatter_dp(self):
        self.grs.wait_recv()
        self.grs.slots[0] = self.part[self.grs.me()]
        total = self.grs.get(0)
        for source in range(1, self.n_g):
            total = total + self.grs.get(source)
        for piece in range(self.n_z):
            self.zsrc[piece] = total[self.place(piece)]
        self.zrs.start(lambda to: self.zsrc.at[to])

    def gather_dp(self):
        self.zrs.wait_recv()
        self.zrs.slots[0] = self.zsrc[self.zrs.me()]
        total = self.zrs.get(0)
        for source in range(1, self.n_z):
            total = total + self.zrs.get(source)
        self.zag.slots[0] = total
        self.zag.start(lambda to: self.zag.slots.at[0])

    def gather_outer(self):
        self.zag.wait_recv()
        for piece in range(self.n_z):
            self.gag.slots[(0, *self.place(piece))] = self.zag.get(piece)
        self.gag.start(lambda to: self.gag.slots.at[0])

    def finish(self):
        self.gag.wait_recv()
        return [self.gag.get(source) for source in range(self.n_g)]

    def drain(self):
        for exchange in (self.grs, self.zrs, self.zag, self.gag):
            exchange.wait_send()


class Pair:
    def __init__(self, to, slot, sems):
        self.to, self.slot, self.sems = to, slot, sems

    def start(self, source):
        pltpu.make_async_remote_copy(
            src_ref=source,
            dst_ref=self.slot,
            send_sem=self.sems.at[0],
            recv_sem=self.sems.at[1],
            device_id={"dp": self.to},
            device_id_type=MESH,
        ).start()

    def wait_recv(self):
        pltpu.make_async_copy(self.slot, self.slot, self.sems.at[1]).wait()

    def wait_send(self):
        pltpu.make_async_copy(self.slot, self.slot, self.sems.at[0]).wait()


class PairReduce(Reduce):
    def __init__(self, n_g, n_z, part, grs, zsrc, zpair, zmid, zrs, zag, zback, gag, sems):
        self.n_g, self.half, self.part, self.zsrc, self.zmid = n_g, n_z // 2, part, zsrc, zmid
        self.height, self.width = zsrc.shape[2:]
        self.across = part.shape[2] // self.width
        shift = lax.rem(lax.axis_index("outer"), 2)
        z = lax.axis_index("dp")
        self.parity = lax.rem(z + shift, 2)
        partner = lax.rem(z + n_z + 1 - 2 * self.parity, n_z)
        self.grs = Exchange("outer", n_g, grs, sems.at[0])
        self.pair = Pair(partner, zpair.at[pl.ds(0, self.half)], sems.at[1])
        self.zrs = Exchange("dp", self.half, zrs, sems.at[2], 2, shift)
        self.zag = Exchange("dp", self.half, zag, sems.at[3], 2, shift)
        self.back = Pair(partner, zback.at[pl.ds(0, self.half)], sems.at[4])
        self.gag = Exchange("outer", n_g, gag, sems.at[5])

    def place(self, piece):
        down, right = piece // self.across * self.height, piece % self.across * self.width
        return slice(down, down + self.height), slice(right, right + self.width)

    def scatter_outer(self):
        self.grs.start(lambda to: self.part.at[to])

    def swap_dp(self):
        self.grs.wait_recv()
        self.grs.slots[0] = self.part[self.grs.me()]
        total = self.grs.get(0)
        for source in range(1, self.n_g):
            total = total + self.grs.get(source)
        for piece in range(2 * self.half):
            self.zsrc[piece % 2, piece // 2] = total[self.place(piece)]
        self.pair.start(self.zsrc.at[1 - self.parity])

    def scatter_dp(self):
        self.pair.wait_recv()
        for piece in range(self.half):
            self.zmid[piece] = self.zsrc[self.parity, piece] + self.pair.slot[piece]
        self.zrs.start(lambda to: self.zmid.at[to])

    def gather_dp(self):
        self.zrs.wait_recv()
        self.zrs.slots[0] = self.zmid[self.zrs.me()]
        total = self.zrs.get(0)
        for source in range(1, self.half):
            total = total + self.zrs.get(source)
        self.zag.slots[0] = total
        self.zag.start(lambda to: self.zag.slots.at[0])

    def swap_back(self):
        self.zag.wait_recv()
        self.back.start(self.zag.slots.at[pl.ds(0, self.half)])

    def gather_outer(self):
        self.back.wait_recv()
        mine = self.zag.me()
        for piece in range(2 * self.half):
            slot = lax.rem(mine + self.half - piece // 2, self.half)
            block = jnp.where(self.parity == piece % 2, self.zag.slots[slot], self.back.slot[slot])
            self.gag.slots[(0, *self.place(piece))] = block
        self.gag.start(lambda to: self.gag.slots.at[0])

    def finish(self):
        self.gag.wait_recv()
        return [self.gag.get(source) for source in range(self.n_g)]

    def drain(self):
        for exchange in (self.grs, self.pair, self.zrs, self.zag, self.back, self.gag):
            exchange.wait_send()


def kernel(
    sizes,
    acts, dy, err, q,
    out, q_out,
    held, dyv, dyall, qv, wsrc, wex, vex, gex, pfull, prow, elim,
    part_p, grs_p, zsrc_p, zrs_p, zag_p, gag_p,
    part_u, grs_u, zsrc_u, zpair_u, zmid_u, zrs_u, zag_u, zback_u, gag_u,
    loc, ring_send, ring_recv, dyz_sems, dyx_sems, wex_sems, vex_sems, gram_sems, p_sems, u_sems,
):
    n_g, n_z, n_x = sizes
    z, x = lax.axis_index("dp"), lax.axis_index("tensor")
    tok, cols = acts.shape
    rows = dy.shape[1]
    rows_z = rows // n_z
    rank = q.shape[0]
    quarter, part = tok // n_x, tok // CHUNKS
    steps = n_z // 2

    loads = [
        pltpu.make_async_copy(src, dst, loc.at[i])
        for i, (src, dst) in enumerate(((acts, held.at[0]), (q, qv), (err, out), (dy, dyv)))
    ]
    for load in loads:
        load.start()
    my_tokens = pl.ds(pl.multiple_of(x * quarter, quarter), quarter)
    own_dy = pltpu.make_async_copy(
        dy.at[my_tokens, pl.ds(pl.multiple_of(z * rows_z, rows_z), rows_z)], dyall.at[0, my_tokens, :], loc.at[4]
    )
    own_dy.start()

    barrier = pltpu.get_barrier_semaphore()
    for axis, n in (("dp", n_z), ("tensor", n_x), ("outer", n_g)):
        def greet(d, carry, axis=axis, n=n):
            to = lax.rem(lax.axis_index(axis) + d, n)
            pl.semaphore_signal(barrier, inc=1, device_id={axis: to}, device_id_type=MESH)
            return carry

        lax.fori_loop(1, n, greet, 0)
    pl.semaphore_wait(barrier, n_z + n_x + n_g - 3)

    def chunk(slot, c):
        return held.at[slot, pl.ds(c * part, part), :]

    def ring_copy(direction, s, c):
        here, there = (s, s + 1) if direction == 0 else ((n_z - s) % n_z, n_z - s - 1)
        to = lax.rem(z + (1 if direction == 0 else n_z - 1), n_z)
        return pltpu.make_async_remote_copy(
            src_ref=acts.at[pl.ds(c * part, part), :] if s == 0 else chunk(here, c),
            dst_ref=chunk(there, c),
            send_sem=ring_send.at[direction, s, c],
            recv_sem=ring_recv.at[direction, s, c],
            device_id={"dp": to},
            device_id_type=MESH,
        )

    def sends(s, c):
        return [ring_copy(direction, s, c) for direction in range(2) if s < steps - 1 or (c < RIGHT) == (direction == 0)]

    for c in range(CHUNKS):
        for copy in sends(0, c):
            copy.start()

    def send_dyz(i, carry):
        d = (i % 2) * ((i + 1) // 2) + (1 - i % 2) * (n_z - i // 2)
        to = lax.rem(z + d, n_z)
        pltpu.make_async_remote_copy(
            src_ref=dy.at[my_tokens, pl.ds(pl.multiple_of(to * rows_z, rows_z), rows_z)],
            dst_ref=dyall.at[d, my_tokens, :],
            send_sem=dyz_sems.at[0],
            recv_sem=dyz_sems.at[1],
            device_id={"dp": to},
            device_id_type=MESH,
        ).start()
        return carry

    def start_dyz():
        lax.fori_loop(1, n_z, send_dyz, 0)

    def wait_dyz(which):
        arrived = dyall.at[pl.ds(1, n_z - 1), pl.ds(0, quarter), :]
        pltpu.make_async_copy(arrived, arrived, dyz_sems.at[which]).wait()

    def send_dyx(piece):
        if piece == 0:
            wait_dyz(1)
            own_dy.wait()

        def send(d, carry):
            mine = dyall.at[pl.ds(piece * steps, steps), my_tokens, :]
            pltpu.make_async_remote_copy(
                src_ref=mine,
                dst_ref=mine,
                send_sem=dyx_sems.at[0, piece],
                recv_sem=dyx_sems.at[1, piece],
                device_id={"tensor": lax.rem(x + d, n_x)},
                device_id_type=MESH,
            ).start()
            return carry

        lax.fori_loop(1, n_x, send, 0)

    def wait_dyx(which):
        for piece in range(2):
            arrived = dyall.at[pl.ds(piece * steps, steps), pl.ds(0, quarter * (n_x - 1)), :]
            pltpu.make_async_copy(arrived, arrived, dyx_sems.at[which, piece]).wait()

    p_sum = Reduce(n_g, n_z, part_p, grs_p, zsrc_p, zrs_p, zag_p, gag_p, p_sems)
    u_sum = PairReduce(n_g, n_z, part_u, grs_u, zsrc_u, zpair_u, zmid_u, zrs_u, zag_u, zback_u, gag_u, u_sems)
    w_exchange = Exchange("tensor", n_x, wex, wex_sems)
    v_exchange = Exchange("tensor", n_x, vex, vex_sems)
    gram_exchange = Exchange("outer", n_g, gex, gram_sems)
    wide = rows // n_g
    my_rows = pl.ds(pl.multiple_of(z * rows_z, rows_z), rows_z)

    def start_w():
        for load in loads[:3]:
            load.wait()
        qt = qv[...]
        wsrc[:, :, :tok] = dot3(qt, held[0], NT).reshape(n_x, rank // n_x, tok)
        wsrc[:, :, tok:] = dot(qt, out[...], NT, HIGH).reshape(n_x, rank // n_x, rows_z)
        w_exchange.start(lambda to: wsrc.at[to])

    def start_p():
        w_exchange.wait_recv()
        loads[3].wait()
        wex[0] = wsrc[x]
        total = w_exchange.get(0)
        for source in range(1, n_x):
            total = total + w_exchange.get(source)
        pt = dot3(total[:, :tok], dyv[...], NN)
        for group in range(n_g):
            part_p[group] = pt[:, group * wide : (group + 1) * wide]
        mine = z * rows_z
        part_p[mine // wide, :, pl.ds(pl.multiple_of(lax.rem(mine, wide), 128), rows_z)] += total[:, tok:]
        p_sum.scatter_outer()

    def gather_p():
        pt = jnp.concatenate(p_sum.finish(), axis=1) * (1.0 / n_g)
        pfull[...] = pt
        vex[0, :, :tok] = dot3(pt, dyv[...], NT)
        vex[0, :, tok : tok + rows_z] = pfull[:, my_rows]
        vex[0, :, tok + rows_z :] = gag_p[0] * (1.0 / n_g)
        v_exchange.start(lambda to: vex.at[0])

    def start_u():
        v_exchange.wait_recv()
        vr = jnp.concatenate([v_exchange.get(source) for source in range(n_x)], axis=0)
        own_rows, some_rows = vr[:, tok : tok + rows_z], vr[:, tok + rows_z :]
        prow[...] = own_rows
        ut = dot3(vr[:, :tok], held[0], NN) + dot(own_rows, out[...], NN, HIGH)
        part_u[...] = ut.reshape(n_g, rank // n_g, cols)
        u_sum.scatter_outer()
        gram = dot(some_rows, some_rows, NT, HIGH)
        gex[0] = jnp.concatenate([gram, jnp.zeros_like(gram)], axis=1)
        gram_exchange.start(lambda to: gex.at[0])

    def start_gram():
        gram_exchange.wait_recv()
        gram = gram_exchange.get(0)
        for source in range(1, n_g):
            gram = gram + gram_exchange.get(source)
        row = lax.broadcasted_iota(jnp.int32, (rank, rank), 0)
        col = lax.broadcasted_iota(jnp.int32, (rank, rank), 1)
        elim[:rank, :rank] = (row == col).astype(F32)
        elim[:rank, rank:] = gram[:, :rank]

    def eliminate(first, last):
        row = lax.broadcasted_iota(jnp.int32, (rank, 2 * rank), 0)
        lane = lax.broadcasted_iota(jnp.int32, (rank, 2 * rank), 1)
        lane1 = lax.broadcasted_iota(jnp.int32, (1, 2 * rank), 1)

        def column(j, carry):
            whole = elim[:rank]
            pivot_row = elim[pl.ds(j, 1), :]
            pivot = jnp.sum(jnp.where(lane1 == rank + j, pivot_row, 0.0), axis=1, keepdims=True)
            scale = 1.0 / jnp.sqrt(pivot)
            pivot_row = pivot_row * scale
            factor = jnp.sum(jnp.where(lane == rank + j, whole, 0.0), axis=1, keepdims=True) * scale
            elim[:rank] = jnp.where(row > j, whole - factor * pivot_row, jnp.where(row == j, pivot_row, whole))
            return carry

        lax.fori_loop(first, last, column, 0)

    def finish_u():
        q_out[...] = jnp.concatenate(u_sum.finish(), axis=0)

    def correct():
        inverse = elim[:rank, :rank]
        qt = dot(inverse, q_out[...], NN, HIGH) * (1.0 / n_g)
        pt = dot(inverse, prow[...], NN, HIGH)
        q_out[...] = qt
        p_hi, q_hi = pt.astype(BF16), qt.astype(BF16)
        p_lo, q_lo = (pt - p_hi.astype(F32)).astype(BF16), (qt - q_hi.astype(F32)).astype(BF16)
        left = jnp.concatenate([p_hi, p_hi, p_lo], axis=0)
        right = jnp.concatenate([q_hi, q_lo, q_hi], axis=0)
        out[...] -= dot(left, right, TN)

    def add(slot):
        out[...] += dot(dyall[slot], held[slot], TN)

    def add_piece(slot, first, count):
        some = pl.ds(first * part, count * part)
        out[...] += dot(dyall[slot, some, :], held[slot, some, :], TN)

    last = CHUNKS * steps - 1
    work = [
        (5, start_p),
        (7, p_sum.scatter_dp),
        (10, p_sum.gather_dp),
        (10, start_dyz),
        (13, p_sum.gather_outer),
        (13, gather_p),
        (13, start_u),
        (15, u_sum.swap_dp),
        (15, start_gram),
        (16, lambda: send_dyx(0)),
        (16, lambda: eliminate(0, rank // 2)),
        (17, lambda: send_dyx(1)),
        (18, u_sum.scatter_dp),
        (20, u_sum.gather_dp),
        (21, lambda: eliminate(rank // 2, rank)),
        (23, lambda: wait_dyx(1)),
        (23, u_sum.swap_back),
        (26, u_sum.gather_outer),
        (28, finish_u),
        (29, correct),
    ]
    order = [0] + [slot for d in range(1, steps) for slot in (d, n_z - d)]
    for i, slot in enumerate(order):
        arrived = CHUNKS * min(slot, n_z - slot) + CHUNKS - 1
        work.append((max(23 + i // 2, arrived), functools.partial(add, slot)))
    work.sort(key=lambda entry: entry[0])

    start_w()
    for t in range(CHUNKS, last + 1):
        s, c = t // CHUNKS, t % CHUNKS
        for copy in sends(s - 1, c):
            copy.wait_recv()
        for copy in sends(s, c):
            copy.start()
        for at, do in work:
            if at == t or (t == last and at > last):
                do()
    for c in range(max(RIGHT, CHUNKS - RIGHT)):
        for first, count in ((c, RIGHT), (RIGHT + c, CHUNKS)):
            if first < count:
                for copy in sends(steps - 1, first):
                    copy.wait_recv()
                add_piece(steps, first, 1)
    for s in range(steps):
        for c in range(CHUNKS):
            for copy in sends(s, c):
                copy.wait_send()
    wait_dyz(0)
    wait_dyx(0)
    w_exchange.wait_send()
    v_exchange.wait_send()
    gram_exchange.wait_send()
    p_sum.drain()
    u_sum.drain()


def store(new_error, q_next, error_out, q_out, sems):
    copies = [
        pltpu.make_async_copy(new_error, error_out, sems.at[0]),
        pltpu.make_async_copy(q_next, q_out, sems.at[1]),
    ]
    for copy in copies:
        copy.start()
    for copy in copies:
        copy.wait()


def local(sizes, acts, out_grads, error, q_warm):
    n_g, n_z, n_x = sizes
    tok, cols = acts.shape
    rows = out_grads.shape[1]
    rows_z = rows // n_z
    rank = q_warm.shape[1]

    def reduce_scratch(height, width, paired):
        across = min(n_z, width // 128)
        piece = (height * across // n_z, width // across)
        whole = pltpu.VMEM((n_g, height, width), F32)
        pieces, half = pltpu.VMEM((n_z + 1, *piece), F32), pltpu.VMEM((n_z // 2 + 1, *piece), F32)
        if paired:
            return [whole, whole, pltpu.VMEM((3, n_z // 2, *piece), F32), *[half] * 5, whole]
        return [whole, whole, *[pieces] * 3, whole]

    anywhere = pl.BlockSpec(memory_space=pl.ANY)
    in_vmem = pl.BlockSpec(memory_space=pltpu.VMEM)
    dma = pltpu.SemaphoreType.DMA
    new_error, q_next = pl.pallas_call(
        functools.partial(kernel, sizes),
        out_shape=(
            pltpu.VMEM((rows_z, cols), F32),
            pltpu.VMEM((rank, cols), F32),
        ),
        in_specs=[anywhere] * 4,
        out_specs=(in_vmem, in_vmem),
        scratch_shapes=[
            pltpu.VMEM((n_z, tok, cols), BF16),
            pltpu.VMEM((tok, rows), BF16),
            pltpu.VMEM((n_z, tok, rows_z), BF16),
            pltpu.VMEM((rank, cols), F32),
            pltpu.VMEM((n_x, rank // n_x, tok + rows_z), F32),
            pltpu.VMEM((n_x, rank // n_x, tok + rows_z), F32),
            pltpu.VMEM((n_x, rank // n_x, tok + rows_z + rows // n_g), F32),
            pltpu.VMEM((n_g, rank, 2 * rank), F32),
            pltpu.VMEM((rank // n_x, rows), F32),
            pltpu.VMEM((rank, rows_z), F32),
            pltpu.VMEM((rank + 8, 2 * rank), F32),
            *reduce_scratch(rank // n_x, rows // n_g, False),
            *reduce_scratch(rank // n_g, cols, True),
            dma((5,)),
            dma((2, n_z // 2, CHUNKS)),
            dma((2, n_z // 2, CHUNKS)),
            dma((2,)),
            dma((2, 2)),
            dma((2,)),
            dma((2,)),
            dma((2,)),
            dma((4, 2)),
            dma((6, 2)),
        ],
        compiler_params=pltpu.CompilerParams(
            collective_id=0, has_side_effects=True, vmem_limit_bytes=48 * 1024 * 1024
        ),
        cost_estimate=pl.CostEstimate(
            flops=2 * rows_z * cols * tok * n_z, bytes_accessed=2 * tok * (cols + rows) + 8 * rows_z * cols, transcendentals=0
        ),
        name="powersgd_step",
    )(*(pltpu.with_memory_space_constraint(a, pltpu.HBM) for a in (acts, out_grads, error[0], q_warm.T)))
    new_error, q_next = pl.pallas_call(
        store,
        out_shape=(
            jax.ShapeDtypeStruct(new_error.shape, F32),
            jax.ShapeDtypeStruct(q_next.shape, F32),
        ),
        in_specs=[in_vmem] * 2,
        out_specs=(anywhere, anywhere),
        scratch_shapes=[dma((2,))],
        name="store_results",
    )(*(pltpu.with_memory_space_constraint(a, pltpu.VMEM) for a in (new_error, q_next)))
    return new_error[None], q_next.T


def solution(mesh):
    sizes = (mesh.shape["outer"], mesh.shape["dp"], mesh.shape["tensor"])
    in_specs = (
        P(("outer", "dp"), "tensor"),
        P(("outer", "dp"), None),
        P("outer", "dp", "tensor"),
        P("tensor", None),
    )
    out_specs = (P("outer", "dp", "tensor"), P("tensor", None))
    return jax.shard_map(
        functools.partial(local, sizes), mesh=mesh, in_specs=in_specs, out_specs=out_specs, check_vma=False
    )
```
